256 devices in a mesh: samp: 64 (over x, z_hi, y, core), tok: 4 (over z_lo).
Axes of the slice: x: 4, y: 4, z: 8 (z_hi: 2, z_lo: 4; z = z_hi * 4 + z_lo), core: 2. Of those that a mesh axis runs over, the one named last changes fastest.
Arguments:
- inputs: bfloat16 [64, 512, 768], P('samp', 'tok'), may hold values from -6 to 6
- cotangent: bfloat16 [64, 512, 768], P('samp', 'tok'), may hold values from -6 to 6
- layer_norm_scale: float32 [768], replicated, may hold values from 0.25 to 1.75
- query_weight: bfloat16 [768, 768], P('samp'), may hold values from -0.3125 to 0.3125
- key_weight: bfloat16 [768, 768], P('samp'), may hold values from -0.3125 to 0.3125
- value_weight: bfloat16 [768, 768], P('samp'), may hold values from -0.21875 to 0.21875
- gate_weight: bfloat16 [768, 768], P('samp'), may hold values from -0.21875 to 0.21875
- out_weight: bfloat16 [768, 768], P('samp'), may hold values from -0.21875 to 0.21875
- pair_bias: bfloat16 [16, 512, 512], P(None, 'tok'), may hold values from -2 to 230
- atom_count: int32 [512], replicated, may hold values from 0 to 7
Outputs:
- input_grad: bfloat16 [64, 512, 768], P('samp', 'tok')
- bias_grad: float32 [16, 512, 512], P(None, 'tok', 'samp')
The draws below stay inside these ranges and needn't reach their ends.
All inputs are finite; a program needn't handle non-finite values.
Results may differ from the reference program's by a relative error of at most 0.019.
Values may be sent and summed in bfloat16 or wider, within the bound.
No kernel may reach another device: no remote copies, remote signals or barrier semaphores. Data moves between devices by JAX's collectives and lax.ppermute only.
A program may use at most 128 MiB of HBM per device.

```python
import jax
import jax.numpy as jnp
from jax import lax

D = 768
HEADS = 16
TOKENS = 512
SAMPLES = 64


def draw_pair_bias(key, part):
    key = jax.random.fold_in(key, 11)
    keyset = jax.random.split(key, 1)
    shape = (HEADS, TOKENS, TOKENS)
    base = jnp.clip(jax.random.normal(keyset[0], shape) * 0.25, -1.5, 1.5)
    return base.astype(jnp.bfloat16)


def place_ends(drawn, key, smallest, top_value):
    place = [jax.random.randint(jax.random.fold_in(key, axis), (), 0, length) for axis, length in enumerate(drawn.shape)]
    longest = drawn.shape.index(max(drawn.shape))
    neighbour = place[:longest] + [(place[longest] + 1) % drawn.shape[longest]] + place[longest + 1:]
    return drawn.at[tuple(place)].set(smallest).at[tuple(neighbour)].set(top_value)


def block_scale(rng, extent, shards, least, top_value):
    gain, own = 1.0, jax.random.fold_in(rng, 6)
    for dim, shards_of in shards:
        steps = jnp.exp(jax.random.uniform(jax.random.fold_in(own, dim), (shards_of,), jnp.float32, least / len(shards), top_value / len(shards)))
        gain = gain * jnp.repeat(steps, extent[dim] // shards_of).reshape([-1 if axis == dim else 1 for axis in range(len(extent))])
    return gain


def normal_values(rng, shape, scale, bound, cuts=(), kind=jnp.bfloat16):
    drawn = jax.random.normal(rng, shape, jnp.float32) * scale
    if len(cuts) > 0:
        drawn = block_scale(rng, shape, cuts, -0.22, 0.18) * drawn
    return jnp.clip(drawn, min=-bound, max=bound).astype(kind)


def setup_inputs(seed: int = 0) -> dict:
    key_list = jax.random.split(jax.random.key(seed), 11)
    inputs = normal_values(key_list[0], (SAMPLES, TOKENS, D), 1.0, 6.0, ((0, 64), (1, 4)))
    cotangent = normal_values(key_list[1], (SAMPLES, TOKENS, D), 1.0, 6.0, ((0, 64), (1, 4)))
    layer_norm_scale = jnp.clip(1.0 + 0.15 * jax.random.normal(key_list[2], (D,), jnp.float32), 0.25, 1.75)
    query_weight = normal_values(key_list[3], (D, D), (D // 2) ** -0.5, 0.3125, ((0, 64),))
    key_weight = normal_values(key_list[4], (D, D), (D // 2) ** -0.5, 0.3125, ((0, 64),))
    value_weight = normal_values(key_list[5], (D, D), D ** -0.5, 0.21875, ((0, 64),))
    gate_weight = normal_values(key_list[6], (D, D), D ** -0.5, 0.21875, ((0, 64),))
    out_weight = normal_values(key_list[7], (D, D), D ** -0.5, 0.21875, ((0, 64),))
    pair_bias = draw_pair_bias(jax.random.fold_in(key_list[10], 71), 0)
    atom_count = place_ends(jax.random.randint(key_list[9], (TOKENS,), 0, 8), jax.random.fold_in(key_list[9], 1), 0, 7).astype(jnp.int32)
    return {"inputs": inputs, "cotangent": cotangent, "layer_norm_scale": layer_norm_scale, "query_weight": query_weight, "key_weight": key_weight, "value_weight": value_weight, "gate_weight": gate_weight, "out_weight": out_weight, "pair_bias": pair_bias, "atom_count": atom_count}


def one_sample(total, pair, layer_norm_scale, query_weight, key_weight, value_weight, gate_weight, out_weight, pair_bias, valid):
    sample_in, sample_cot = pair
    heads = pair_bias.shape[0]
    tokens, width = sample_in.shape
    head_size = width // heads
    scale = float(head_size) ** (-0.5)
    xf = sample_in.astype(jnp.float32)
    row_average = lax.optimization_barrier(jnp.mean(xf, axis=-1, keepdims=True))
    centered_rows = xf - row_average
    inverse_deviation = lax.rsqrt(lax.optimization_barrier(jnp.mean(centered_rows * centered_rows, axis=-1, keepdims=True)) + 1e-05)
    standardized_input = centered_rows * inverse_deviation
    normed_output = (standardized_input * layer_norm_scale).astype(jnp.bfloat16)
    query = jnp.dot(normed_output, query_weight, preferred_element_type=jnp.float32).astype(jnp.bfloat16)
    keys = jnp.dot(normed_output, key_weight, preferred_element_type=jnp.float32).astype(jnp.bfloat16)
    values = jnp.dot(normed_output, value_weight, preferred_element_type=jnp.float32).astype(jnp.bfloat16)
    gate_pre = jnp.dot(normed_output, gate_weight, preferred_element_type=jnp.float32).astype(jnp.bfloat16)
    d_gated = jnp.dot(sample_cot, out_weight.T, preferred_element_type=jnp.float32)
    sigma = jax.nn.sigmoid(gate_pre.astype(jnp.float32))
    d_attn = (d_gated * sigma).astype(jnp.bfloat16)
    qh = query.astype(jnp.float32).reshape(tokens, heads, head_size)
    kh = keys.astype(jnp.float32).reshape(tokens, heads, head_size)
    vh = values.astype(jnp.float32).reshape(tokens, heads, head_size)
    dh = d_attn.astype(jnp.float32).reshape(tokens, heads, head_size)
    scores = jnp.einsum('qhe,khe->hqk', qh, kh) * scale + pair_bias.astype(jnp.float32)
    scores = jnp.where(valid[None, None, :], scores, -1000000000.0)
    probs = jax.nn.softmax(scores, axis=-1)
    probs_b = probs.astype(jnp.bfloat16).astype(jnp.float32)
    attended = jnp.einsum('hqk,khe->qhe', probs_b, vh).astype(jnp.bfloat16)
    delta = lax.optimization_barrier(jnp.sum(dh * attended.astype(jnp.float32), axis=-1))
    d_prob = jnp.einsum('qhe,khe->hqk', dh, vh)
    d_score = probs * (d_prob - jnp.transpose(delta)[:, :, None])
    d_score_b = d_score.astype(jnp.bfloat16).astype(jnp.float32)
    d_query = (jnp.einsum('hqk,khe->qhe', d_score_b, kh) * scale).astype(jnp.bfloat16).reshape(tokens, width)
    d_keys = (jnp.einsum('hqk,qhe->khe', d_score_b, qh) * scale).reshape(tokens, width).astype(jnp.bfloat16)
    d_values = jnp.einsum('hqk,qhe->khe', probs_b, dh).reshape(tokens, width).astype(jnp.bfloat16)
    attended_flat = attended.reshape(tokens, width).astype(jnp.float32)
    d_gate = (d_gated * attended_flat * sigma * (1.0 - sigma)).astype(jnp.bfloat16)
    d_normed = jnp.dot(d_query, query_weight.T, preferred_element_type=jnp.float32)
    d_normed = d_normed + jnp.dot(d_gate, gate_weight.T, preferred_element_type=jnp.float32)
    d_normed = d_normed + jnp.dot(d_keys, key_weight.T, preferred_element_type=jnp.float32)
    d_normed = d_normed + jnp.dot(d_values, value_weight.T, preferred_element_type=jnp.float32)
    upstream_gradient = d_normed * layer_norm_scale
    final_output = inverse_deviation * (upstream_gradient - lax.optimization_barrier(jnp.mean(upstream_gradient, axis=-1, keepdims=True)) - standardized_input * lax.optimization_barrier(jnp.mean(upstream_gradient * standardized_input, axis=-1, keepdims=True)))
    return (total + d_score, final_output.astype(jnp.bfloat16))

def reference(inputs, cotangent, layer_norm_scale, query_weight, key_weight, value_weight, gate_weight, out_weight, pair_bias, atom_count):
    valid = atom_count > 0
    start = jnp.zeros(pair_bias.shape, jnp.float32)

    def step(total, pair):
        return one_sample(total, pair, layer_norm_scale, query_weight, key_weight, value_weight, gate_weight, out_weight, pair_bias, valid)
    bias_grad, input_grad = lax.scan(step, start, (inputs, cotangent))
    return (input_grad, bias_grad)
```

```python
import jax
import jax.numpy as jnp
from jax import lax
from jax.experimental import pallas as pl
from jax.experimental.pallas import tpu as pltpu
from jax.sharding import Mesh, PartitionSpec as P

AXES = (("x", 4), ("zh", 2), ("y", 4), ("core", 2))
NX, NZ, NY, NC = 4, 2, 4, 2
NT = 4
BF = jnp.bfloat16
F32 = jnp.float32
NEG = -1000000000.0


def shift(value, axis, count, by):
    return lax.ppermute(value, axis, [(i, (i + by) % count) for i in range(count)])


def nt(a, b):
    return lax.dot_general(a, b, (((1,), (1,)), ((), ())), preferred_element_type=F32)


def nn(a, b):
    return lax.dot_general(a, b, (((1,), (0,)), ((), ())), preferred_element_type=F32)


def attention_kernel(
    pos,
    own0, own1, own2, own3,
    oth0, oth1, oth2, oth3,
    cot_own, cot_oth,
    a0, a1, a2, a3,
    b0, b1, b2, b3,
    bias, valid_row, valid_col,
    out_own, out_oth, out_bias,
    wf, wb, dgt, kk, vv, kt, vt, qt, gt, dx, dq, dg, grad,
):
    heads = bias.shape[0] // NC
    width = own0.shape[1]
    half = width // NC
    size = half // heads
    rows = own0.shape[0]
    scale = float(size) ** (-0.5)
    x, y, core, tok = pos[0], pos[1], pos[2], pos[3]
    rx, rz, ry = width // NX, width // (NX * NZ), width // (NX * NZ * NY)
    piece = NZ * ry

    for m, (a, b) in enumerate(zip((a0, a1, a2, a3), (b0, b1, b2, b3))):
        for k in range(4):
            rows_a = a[k * piece:(k + 1) * piece, :].astype(F32)
            rows_b = b[k * piece:(k + 1) * piece, :half].astype(F32)
            for z in range(NZ):
                at_a = lax.rem(x - k + 4, 4) * rx + z * rz + lax.rem(y - m + 4, 4) * ry
                wf[pl.ds(pl.multiple_of(at_a, 8), ry), : 3 * half] = rows_a[z * ry:(z + 1) * ry]
                at_b = lax.rem(x - m + 4, 4) * rx + z * rz + lax.rem(y - k + 4, 4) * ry
                wf[pl.ds(pl.multiple_of(at_b, 8), ry), 3 * half:] = rows_b[z * ry:(z + 1) * ry]
    wb[...] = wf[...].astype(BF)

    for s, cot in enumerate((cot_own, cot_oth)):
        for m, b in enumerate((b0, b1, b2, b3)):
            part = nt(b[:, half:], cot[...])
            for k in range(4):
                for z in range(NZ):
                    at = lax.rem(x - m + 4, 4) * rx + z * rz + lax.rem(y - k + 4, 4) * ry
                    dgt[s, pl.ds(pl.multiple_of(at, 8), ry), :] = part[k * piece + z * ry:k * piece + (z + 1) * ry]

    for s, blocks in enumerate(((own0, own1, own2, own3), (oth0, oth1, oth2, oth3))):
        for r, block in enumerate(blocks):
            lo = r * rows
            n = block[...]
            k_f = nn(n, wb[:, half:2 * half])
            v_f = nn(n, wb[:, 2 * half:3 * half])
            kt[s, :, lo:lo + rows] = k_f.T.astype(BF)
            vt[s, :, lo:lo + rows] = v_f.T.astype(BF)
            at = pl.multiple_of(lax.rem(tok - r + 4, 4) * rows, rows)
            keep = valid_col[pl.ds(at, rows), :]
            for j in range(half // 128):
                kk[s, lo:lo + rows, j * 128:(j + 1) * 128] = (k_f[:, j * 128:(j + 1) * 128] * keep).astype(BF)
            vv[s, lo:lo + rows, :] = v_f.astype(BF)
        n = blocks[0][...]
        qt[s] = nn(n, wb[:, :half]).T.astype(BF)
        gate = nn(n, wb[:, 3 * half:]).T.astype(BF).astype(F32)
        gt[s] = jax.nn.sigmoid(gate)

    for h in range(heads):
        first = h * size
        w_lo = first // 128 * 128
        w_hi = -(-(first + size) // 128) * 128
        above, below = first - w_lo, w_hi - first - size

        def widen(block):
            parts = [block]
            if above:
                parts = [jnp.zeros((above, rows), BF)] + parts
            if below:
                parts = parts + [jnp.zeros((below, rows), BF)]
            return jnp.concatenate(parts, axis=0) if len(parts) > 1 else block

        masked = jnp.where(valid_row[...] > 0.0, bias[core * heads + h].astype(F32), NEG)
        grad[...] = masked.T
        bias_t = jnp.concatenate(
            [grad[pl.ds(pl.multiple_of(lax.rem(tok - r + 4, 4) * rows, rows), rows), :] for r in range(NT)], axis=0
        )
        total = None
        for s in range(2):
            q_h = qt[s, first:first + size, :]
            dgated = dgt[s, pl.ds(pl.multiple_of(core * half + first, 8), size), :]
            sig = gt[s, first:first + size, :]
            da_h = (dgated * sig).astype(BF)
            scores = nn(kk[s, :, w_lo:w_hi], widen(q_h)) * scale + bias_t
            top = jnp.max(scores, axis=0, keepdims=True)
            e = jnp.exp(scores - top)
            probs = e / jnp.sum(e, axis=0, keepdims=True)
            probs_b = probs.astype(BF)
            att = nn(vt[s, first:first + size, :], probs_b).astype(BF).astype(F32)
            delta = jnp.sum(da_h.astype(F32) * att, axis=0, keepdims=True)
            d_prob = nn(vv[s, :, w_lo:w_hi], widen(da_h))
            d_score = probs * (d_prob - delta)
            total = d_score if total is None else total + d_score
            ds_b = d_score.astype(BF)
            dq[s, first:first + size, :] = (nn(kt[s, first:first + size, :], ds_b) * scale).astype(BF)
            dx[s, first:first + size, :] = (nt(q_h, ds_b) * scale).astype(BF)
            dx[s, half + first:half + first + size, :] = nt(da_h, probs_b).astype(BF)
            dg[s, first:first + size, :] = (dgated * att * sig * (1.0 - sig)).astype(BF)
        for r in range(NT):
            to_x = lax.rem(tok - r + 4, 4)
            for z in range(NZ):
                for to_y in range(NY):
                    lo = r * rows + z * (rows // NZ) + to_y * (rows // (NZ * NY))
                    out_bias[to_x * NY + to_y, h, z] = total[lo:lo + rows // (NZ * NY), :].astype(BF)

    for s, out in enumerate((out_own, out_oth)):
        for r in range(NT):
            lo = r * rows
            d = nn(wb[:, half:3 * half], dx[s, :, lo:lo + rows])
            if r == 0:
                d = d + nn(wb[:, :half], dq[s]) + nn(wb[:, 3 * half:], dg[s])
            out[r] = d.astype(out.dtype)


def final_kernel(inputs, gain, d_own, d_oth, r1, r2, r3, out):
    d = d_own[...] + d_oth[...].astype(F32)
    d = d + r1[...].astype(F32) + r2[...].astype(F32) + r3[...].astype(F32)
    g = d.T * gain[...]
    xf = inputs[...].astype(F32)
    mean = jnp.mean(xf, axis=-1, keepdims=True)
    centered = xf - mean
    inv = lax.rsqrt(jnp.mean(centered * centered, axis=-1, keepdims=True) + 1e-05)
    xhat = centered * inv
    res = inv * (g - jnp.mean(g, axis=-1, keepdims=True) - xhat * jnp.mean(g * xhat, axis=-1, keepdims=True))
    out[...] = res.astype(BF)


def on_device(
    inputs,
    cotangent,
    layer_norm_scale,
    query_weight,
    key_weight,
    value_weight,
    gate_weight,
    out_weight,
    pair_bias,
    atom_count,
):
    x, zh, y, core, tok = (lax.axis_index(a) for a in ("x", "zh", "y", "core", "tok"))
    inputs, cotangent = inputs[0], cotangent[0]
    rows, width = inputs.shape
    half = width // NC
    heads = pair_bias.shape[0] // NC
    total = pair_bias.shape[2]

    four = (query_weight, key_weight, value_weight, gate_weight)
    low = jnp.concatenate([w[:, :half] for w in four] + [out_weight], axis=1)
    high = jnp.concatenate([w[:, half:] for w in four] + [out_weight], axis=1)
    mine = jnp.where(core == 0, low, high)
    his = shift(jnp.where(core == 0, high, low), "core", NC, 1)
    pair = jnp.where(core == 0, jnp.stack([mine, his]), jnp.stack([his, mine]))
    far = shift(pair, "zh", NZ, 1)
    quad = jnp.where(zh == 0, jnp.stack([pair, far]), jnp.stack([far, pair]))
    quad = quad.reshape(-1, quad.shape[-1])
    part_a, part_b = quad[:, : 3 * half], quad[:, 3 * half:]
    row_a = jnp.concatenate([part_a] + [shift(part_a, "x", NX, k) for k in (1, 2, 3)], axis=0)
    row_b = jnp.concatenate([part_b] + [shift(part_b, "y", NY, k) for k in (1, 2, 3)], axis=0)
    all_a = [row_a] + [shift(row_a, "y", NY, k) for k in (1, 2, 3)]
    all_b = [row_b] + [shift(row_b, "x", NX, k) for k in (1, 2, 3)]

    xf = inputs.astype(F32)
    mean = jnp.mean(xf, axis=-1, keepdims=True)
    centered = xf - mean
    inv = lax.rsqrt(jnp.mean(centered * centered, axis=-1, keepdims=True) + 1e-05)
    normed = (centered * inv * layer_norm_scale).astype(BF)
    own = [normed] + [shift(normed, "tok", NT, k) for k in (1, 2, 3)]
    oth = [shift(n, "core", NC, 1) for n in own]
    cot_oth = shift(cotangent, "core", NC, 1)

    valid = (atom_count > 0).astype(F32)
    pos = jnp.stack([x, y, core, tok]).astype(jnp.int32)
    vmem = pl.BlockSpec(memory_space=pltpu.VMEM)
    operands = own + oth + [cotangent, cot_oth] + all_a + all_b
    operands += [pair_bias, valid[None, :], jnp.broadcast_to(valid[:, None], (total, 128))]
    out_own, out_oth, out_bias = pl.pallas_call(
        attention_kernel,
        out_shape=(
            jax.ShapeDtypeStruct((NT, width, rows), F32),
            jax.ShapeDtypeStruct((NT, width, rows), BF),
            jax.ShapeDtypeStruct((NX * NY, heads, NZ, rows // (NZ * NY), rows), BF),
        ),
        in_specs=[pl.BlockSpec(memory_space=pltpu.SMEM)] + [vmem] * len(operands),
        out_specs=(vmem, vmem, vmem),
        scratch_shapes=[
            pltpu.VMEM((width, 4 * half), F32),
            pltpu.VMEM((width, 4 * half), BF),
            pltpu.VMEM((2, width, rows), F32),
            pltpu.VMEM((2, total, half), BF),
            pltpu.VMEM((2, total, half), BF),
            pltpu.VMEM((2, half, total), BF),
            pltpu.VMEM((2, half, total), BF),
            pltpu.VMEM((2, half, rows), BF),
            pltpu.VMEM((2, half, rows), F32),
            pltpu.VMEM((2, 2 * half, total), BF),
            pltpu.VMEM((2, half, rows), BF),
            pltpu.VMEM((2, half, rows), BF),
            pltpu.VMEM((total, rows), F32),
        ],
        compiler_params=pltpu.CompilerParams(vmem_limit_bytes=50 * 1024 * 1024),
        name="attention",
    )(pos, *operands)

    d_oth = shift(out_oth, "core", NC, 1)
    back = [
        lax.ppermute(
            (out_own[k] + d_oth[k].astype(F32)).astype(BF), "tok", [(i, (i - k) % NT) for i in range(NT)]
        )
        for k in (1, 2, 3)
    ]

    parts = lax.all_to_all(out_bias, ("x", "y"), 0, 0, tiled=True)
    plane = jnp.sum(parts.astype(F32), axis=0)
    keep = jnp.where(zh == 0, plane[:, 0], plane[:, 1])
    send = jnp.where(zh == 0, plane[:, 1], plane[:, 0])
    summed = keep + shift(send, "zh", NZ, 1)
    per = summed.shape[1] // NC
    keep = jnp.where(core == 0, summed[:, :per], summed[:, per:])
    got = shift(jnp.where(core == 0, summed[:, per:], summed[:, :per]), "core", NC, 1)
    grads = jnp.where(core == 0, jnp.concatenate([keep, got]), jnp.concatenate([got, keep]))
    bias_grad = jnp.transpose(grads, (0, 2, 1))

    input_grad = pl.pallas_call(
        final_kernel,
        out_shape=jax.ShapeDtypeStruct((rows, width), BF),
        in_specs=[vmem] * 7,
        out_specs=vmem,
        compiler_params=pltpu.CompilerParams(vmem_limit_bytes=50 * 1024 * 1024),
        name="norm_back",
    )(inputs, layer_norm_scale[None, :], out_own[0], d_oth[0], *back)
    return input_grad[None], bias_grad


def solution(mesh):
    names = tuple(name for name, _ in AXES)
    split = Mesh(mesh.devices.reshape(tuple(n for _, n in AXES) + (NT,)), names + ("tok",))
    return jax.shard_map(
        on_device,
        mesh=split,
        in_specs=(
            P(names, "tok", None),
            P(names, "tok", None),
            P(),
            P(names, None),
            P(names, None),
            P(names, None),
            P(names, None),
            P(names, None),
            P(None, "tok", None),
            P(),
        ),
        out_specs=(P(names, "tok", None), P(None, "tok", names)),
        check_vma=False,
    )
```

```python
import jax
import jax.numpy as jnp
from jax import lax
from jax.experimental import pallas as pl
from jax.experimental.pallas import tpu as pltpu
from jax.sharding import Mesh, PartitionSpec as P

AXES = (("x", 4), ("zh", 2), ("y", 4), ("core", 2))
TOK = (("th", 2), ("tl", 2))
NX, NZ, NY, NC = 4, 2, 4, 2
NT = 4
BF = jnp.bfloat16
F32 = jnp.float32
NEG = -1000000000.0


def shift(value, axis, count, by):
    return lax.ppermute(value, axis, [(i, (i + by) % count) for i in range(count)])


def swap(value, by):
    return lax.ppermute(value, ("th", "tl"), [(i, i ^ by) for i in range(NT)])


def nt(a, b):
    return lax.dot_general(a, b, (((1,), (1,)), ((), ())), preferred_element_type=F32)


def nn(a, b):
    return lax.dot_general(a, b, (((1,), (0,)), ((), ())), preferred_element_type=F32)


def attention_kernel(
    pos,
    own_near, own_far, oth_near, oth_far,
    cot_own0, cot_own1, cot_oth0, cot_oth1,
    weights,
    bias, bias_pair, valid_row, valid_col,
    out_first, out_own, out_oth, out_bias,
    wf, wo, wb, dgt, kv, km, kvt, qt, gt, dx, dqg,
):
    heads = bias_pair.shape[0]
    width = own_near.shape[1]
    part = width // 4
    size = part // heads
    rows = bias.shape[1]
    scale = float(size) ** (-0.5)
    core, tok, pair = pos[2], pos[3], pos[5]
    rx, rz, ry = width // NX, width // (NX * NZ), width // (NX * NZ * NY)
    tail = weights.shape[2] - width

    for block in range(NX * NY):
        to_x, to_y = divmod(block, NY)
        rows_of = weights[block].astype(F32)
        for z in range(NZ):
            at = to_x * rx + z * rz + to_y * ry
            wf[at:at + ry, :] = rows_of[z * ry:(z + 1) * ry, :width]
            at = to_x * rz + to_y * ry
            wo[at:at + ry, z * tail:(z + 1) * tail] = rows_of[z * ry:(z + 1) * ry, width:]
    wb[...] = wf[...].astype(BF)

    mine = jnp.concatenate(
        [wo[pl.ds(pl.multiple_of(j * rz + pair * size, 8), size), :] for j in range(heads)], axis=0
    ).astype(BF)
    for s, cots in enumerate(((cot_own0, cot_own1), (cot_oth0, cot_oth1))):
        for u, cot in enumerate(cots):
            dgt[s, :, u * rows:(u + 1) * rows] = nt(mine, cot[...])

    for s, tokens in enumerate(((own_near, own_far), (oth_near, oth_far))):
        for r in range(NT):
            n = tokens[r // 2][r % 2 * rows:(r % 2 + 1) * rows, :]
            lo = pl.multiple_of((tok ^ r) * rows, rows)
            both = nn(n, wb[:, : 2 * part])
            kvt[s, :, pl.ds(lo, rows)] = both.T.astype(BF)
            kv[s, pl.ds(lo, rows), :] = both.astype(BF)
            keep = valid_col[pl.ds(lo, rows), :]
            for j in range(2):
                km[s, pl.ds(lo, rows), j * 128:(j + 1) * 128] = (both[:, j * 128:(j + 1) * 128] * keep).astype(BF)
        both = nn(tokens[0][...], wb[:, 2 * part:]).T
        qt[s] = both[:part].astype(BF)
        gt[s] = jax.nn.sigmoid(both[part:].astype(BF).astype(F32))

    def widen(block, first):
        low = first // 128 * 128
        high = -(-(first + size) // 128) * 128
        parts = [block]
        if first > low:
            parts = [jnp.zeros((first - low, block.shape[1]), BF)] + parts
        if high > first + size:
            parts = parts + [jnp.zeros((high - first - size, block.shape[1]), BF)]
        return low, high, jnp.concatenate(parts, axis=0)

    for h in range(heads):
        first = h * size
        at = slice(first, first + size)
        biases = (bias[4 * h + 2 * core + pair], bias_pair[h])
        bias_t = jnp.concatenate(
            [jnp.where(valid_row[...] > 0.0, b.astype(F32), NEG).T for b in biases], axis=1
        )
        total = None
        for s in range(2):
            q_h = qt[s, at, :]
            dgated = dgt[s, at, :]
            sig = gt[s, at, :]
            da_h = (dgated * sig).astype(BF)
            low, high, q_wide = widen(q_h, first)
            scores = nn(km[s, :, low:high], q_wide) * scale + bias_t
            top = jnp.max(scores, axis=0, keepdims=True)
            e = jnp.exp(scores - top)
            probs = e * (1.0 / jnp.sum(e, axis=0, keepdims=True))
            probs_b = probs.astype(BF)
            att = nn(kvt[s, part + first:part + first + size, :], probs_b).astype(BF).astype(F32)
            delta = jnp.sum(da_h.astype(F32) * att, axis=0, keepdims=True)
            low, high, da_wide = widen(da_h, part + first)
            d_prob = nn(kv[s, :, low:high], da_wide)
            d_score = probs * (d_prob - delta)
            total = d_score if total is None else total + d_score
            ds_b = d_score.astype(BF)
            dqg[s, at, :] = (nn(kvt[s, at, :], ds_b) * scale).astype(BF)
            dqg[s, part + first:part + first + size, :] = (dgated * att * sig * (1.0 - sig)).astype(BF)
            dx[s, at, :] = (nt(q_h, ds_b) * scale).astype(BF)
            dx[s, part + first:part + first + size, :] = nt(da_h, probs_b).astype(BF)
        each = rows // (NZ * NY)
        for to_x in range(NX):
            for z in range(NZ):
                for to_y in range(NY):
                    lo = to_x * rows + z * (rows // NZ) + to_y * each
                    out_bias[to_x * NY + to_y, h, z] = total[lo:lo + each, :].astype(BF)

    for s in range(2):
        for r in range(NT):
            at = pl.multiple_of((tok ^ r) * rows, rows)
            d = nn(wb[:, : 2 * part], dx[s, :, pl.ds(at, rows)])
            if r < 2:
                d = d + nn(wb[:, 2 * part:], dqg[s, :, r * rows:(r + 1) * rows])
            if s == 1:
                out_oth[r] = d.astype(BF)
            elif r == 0:
                out_first[...] = d
            else:
                out_own[r - 1] = d.astype(BF)


def pack_kernel(pos, query, key, value, gate, out, mine, send):
    width = query.shape[1]
    part = width // 4
    size = part // NX
    row = lax.broadcasted_iota(jnp.int32, (width, part), 0)
    lane = lax.broadcasted_iota(jnp.int32, (width, part), 1)
    col = lane + pos[5] * size
    for k in range(1, NX):
        col = col + jnp.where(lane >= k * size, width // NX - size, 0)
    low = jnp.where(row == col, 1.0, 0.0).astype(BF)
    high = jnp.where(row == col + 2 * size, 1.0, 0.0).astype(BF)
    first = pos[2] == 0
    lows = jnp.concatenate([nn(w[...], low) for w in (key, value, query, gate)], axis=1)
    highs = jnp.concatenate([nn(w[...], high) for w in (key, value, query, gate)], axis=1)
    mine[:, :width] = jnp.where(first, lows, highs).astype(BF)
    send[:, :width] = jnp.where(first, highs, lows).astype(BF)
    mine[:, width:] = out[...]
    send[:, width:] = out[...]


def norm_kernel(inputs, gain, normed):
    xf = inputs[...].astype(F32)
    centered = xf - jnp.mean(xf, axis=-1, keepdims=True)
    inv = lax.rsqrt(jnp.mean(centered * centered, axis=-1, keepdims=True) + 1e-05)
    normed[...] = (centered * inv * gain[...][None, :]).astype(BF)


def assemble_kernel(pos, mine, beside, above, across, normed, beyond, part, near):
    rows = normed.shape[0]
    near[:rows, :] = normed[...]
    near[rows:, :] = beyond[...]
    first, below = pos[2] == 0, pos[4] == 0
    m, b, u, d = (ref[...].astype(F32) for ref in (mine, beside, above, across))
    near_lo, near_hi = jnp.where(first, m, b), jnp.where(first, b, m)
    far_lo, far_hi = jnp.where(first, u, d), jnp.where(first, d, u)
    cols = normed.shape[1]
    half = part.shape[2] - cols
    quad = jnp.concatenate(
        [
            jnp.where(below, near_lo, far_lo)[:, :cols],
            jnp.where(below, near_hi, far_hi)[:, :cols],
            jnp.where(below, far_lo, near_lo)[:, :cols],
            jnp.where(below, far_hi, near_hi)[:, :cols],
        ],
        axis=0,
    ).astype(BF)
    same = pos[4] == pos[2]
    out_lo, out_hi = jnp.where(same, near_lo, far_lo), jnp.where(same, near_hi, far_hi)
    tail = jnp.concatenate(
        [out_lo[:, cols:cols + half], out_hi[:, cols:cols + half], out_lo[:, cols + half:], out_hi[:, cols + half:]], axis=0
    ).astype(BF)
    for k in range(part.shape[0]):
        part[k, :, :cols] = quad
        part[k, :, cols:] = tail


def sum_kernel(first, own, oth, s0, s1, s2, s3):
    s0[...] = first[...] + oth[0].astype(F32)
    for k, out in enumerate((s1, s2, s3)):
        out[...] = (own[k].astype(F32) + oth[k + 1].astype(F32)).astype(BF)


def plane_kernel(pos, parts, r1, r2, r3, out):
    rows = out.shape[-1]
    each = out.shape[-2]
    total = jnp.sum(parts[...].astype(F32), axis=0)
    for z in range(NZ):
        for c in range(NC):
            for u in range(2):
                out[z, c, pos[5] ^ u] = total[:, z, c * each:(c + 1) * each, u * rows:(u + 1) * rows]


def final_kernel(inputs, gain, r0, r1, r2, r3, out):
    d = r0[...] + r1[...].astype(F32) + r2[...].astype(F32) + r3[...].astype(F32)
    g = d.T * gain[...][None, :]
    xf = inputs[...].astype(F32)
    mean = jnp.mean(xf, axis=-1, keepdims=True)
    centered = xf - mean
    inv = lax.rsqrt(jnp.mean(centered * centered, axis=-1, keepdims=True) + 1e-05)
    xhat = centered * inv
    res = inv * (g - jnp.mean(g, axis=-1, keepdims=True) - xhat * jnp.mean(g * xhat, axis=-1, keepdims=True))
    out[...] = res.astype(BF)


def on_device(
    inputs,
    cotangent,
    layer_norm_scale,
    query_weight,
    key_weight,
    value_weight,
    gate_weight,
    out_weight,
    pair_bias,
    atom_count,
):
    x, zh, y, core, th, tl = (lax.axis_index(a) for a in ("x", "zh", "y", "core", "th", "tl"))
    inputs, cotangent = inputs[0], cotangent[0]
    rows, width = inputs.shape
    part = width // 4
    heads = pair_bias.shape[0] // 4
    total = pair_bias.shape[2]

    pos = jnp.stack([x, y, core, 2 * th + tl, zh, tl]).astype(jnp.int32)
    vmem = pl.BlockSpec(memory_space=pltpu.VMEM)
    smem = pl.BlockSpec(memory_space=pltpu.SMEM)
    anywhere = pl.BlockSpec(memory_space=pl.ANY)
    gain = layer_norm_scale

    packed = jax.ShapeDtypeStruct((query_weight.shape[0], 2 * width), BF)
    mine, send = pl.pallas_call(
        pack_kernel,
        out_shape=(packed, packed),
        in_specs=[smem] + [vmem] * 5,
        out_specs=(vmem, vmem),
        name="pack",
    )(pos, query_weight, key_weight, value_weight, gate_weight, out_weight)
    beside = shift(send, "core", NC, 1)
    above = shift(mine, "zh", NZ, 1)
    across = lax.ppermute(send, ("zh", "core"), [(0, 3), (3, 0), (1, 2), (2, 1)])

    normed = pl.pallas_call(
        norm_kernel,
        out_shape=jax.ShapeDtypeStruct((rows, width), BF),
        in_specs=[vmem, vmem],
        out_specs=vmem,
        name="norm",
    )(inputs, gain)
    beyond = swap(normed, 1)

    pieces, own_near = pl.pallas_call(
        assemble_kernel,
        out_shape=(
            jax.ShapeDtypeStruct((NX * NY, NC * NZ * mine.shape[0], width + width // 2), BF),
            jax.ShapeDtypeStruct((2 * rows, width), BF),
        ),
        in_specs=[smem] + [vmem] * 6,
        out_specs=(vmem, vmem),
        compiler_params=pltpu.CompilerParams(vmem_limit_bytes=30 * 1024 * 1024),
        name="assemble",
    )(pos, mine, beside, above, across, normed, beyond)
    own_far = swap(own_near, 2)
    weights = lax.all_to_all(pieces, ("x", "y"), 0, 0, tiled=True)
    oth_near, oth_far = shift(own_near, "core", NC, 1), shift(own_far, "core", NC, 1)
    cot_pair = swap(cotangent, 1)
    cots = [cotangent, cot_pair, shift(cotangent, "core", NC, 1), shift(cot_pair, "core", NC, 1)]
    groups = pair_bias.reshape((heads, NC, 2) + pair_bias.shape[1:])
    theirs = lax.dynamic_index_in_dim(lax.dynamic_index_in_dim(groups, core, 1, False), 1 - tl, 1, False)
    bias_pair = swap(theirs, 1)

    valid = (atom_count > 0).astype(F32)
    operands = [own_near, own_far, oth_near, oth_far] + cots + [weights]
    operands += [pair_bias, bias_pair, valid[None, :], jnp.broadcast_to(valid[:, None], (total, 128))]
    out_first, out_own, out_oth, out_bias = pl.pallas_call(
        attention_kernel,
        out_shape=(
            jax.ShapeDtypeStruct((width, rows), F32),
            jax.ShapeDtypeStruct((NT - 1, width, rows), BF),
            jax.ShapeDtypeStruct((NT, width, rows), BF),
            jax.ShapeDtypeStruct((NX * NY, heads, NZ, rows // (NZ * NY), 2 * rows), BF),
        ),
        in_specs=[smem] + [vmem] * len(operands),
        out_specs=(vmem,) * 4,
        scratch_shapes=[
            pltpu.VMEM((width, width), F32),
            pltpu.VMEM((width // 2, width), F32),
            pltpu.VMEM((width, width), BF),
            pltpu.VMEM((2, part, 2 * rows), F32),
            pltpu.VMEM((2, total, 2 * part), BF),
            pltpu.VMEM((2, total, 256), BF),
            pltpu.VMEM((2, 2 * part, total), BF),
            pltpu.VMEM((2, part, 2 * rows), BF),
            pltpu.VMEM((2, part, 2 * rows), F32),
            pltpu.VMEM((2, 2 * part, total), BF),
            pltpu.VMEM((2, 2 * part, 2 * rows), BF),
        ],
        compiler_params=pltpu.CompilerParams(vmem_limit_bytes=50 * 1024 * 1024),
        name="attention",
    )(pos, *operands)

    d_oth = shift(out_oth, "core", NC, 1)
    block = jax.ShapeDtypeStruct((width, rows), BF)
    sums = pl.pallas_call(
        sum_kernel,
        out_shape=(jax.ShapeDtypeStruct((width, rows), F32), block, block, block),
        in_specs=[vmem] * 3,
        out_specs=(vmem,) * 4,
        name="sum_cores",
    )(out_first, out_own, d_oth)
    back = [swap(sums[k], k) for k in (1, 2, 3)]

    parts = lax.all_to_all(out_bias, ("x", "y"), 0, 0, tiled=True)
    planes = pl.pallas_call(
        plane_kernel,
        out_shape=jax.ShapeDtypeStruct((NZ, NC, 2, heads, rows // (NZ * NY) // NC, rows), F32),
        in_specs=[smem, vmem, anywhere, anywhere, anywhere],
        out_specs=vmem,
        name="sum_plane",
    )(pos, parts, *back)
    shape = planes.shape
    planes = lax.all_to_all(planes.reshape((-1,) + shape[3:]), ("zh", "core", "tl"), 0, 0, tiled=True)
    planes = jnp.sum(planes.reshape(shape), axis=0)
    bias_grad = jnp.transpose(planes, (2, 0, 1, 4, 3)).reshape(4 * heads, rows, shape[4])

    input_grad = pl.pallas_call(
        final_kernel,
        out_shape=jax.ShapeDtypeStruct((rows, width), BF),
        in_specs=[vmem] * 6,
        out_specs=vmem,
        compiler_params=pltpu.CompilerParams(vmem_limit_bytes=50 * 1024 * 1024),
        name="norm_back",
    )(inputs, gain, sums[0], *back)
    return input_grad[None], bias_grad


def solution(mesh):
    names, toks = tuple(name for name, _ in AXES), tuple(name for name, _ in TOK)
    split = Mesh(mesh.devices.reshape(tuple(n for _, n in AXES + TOK)), names + toks)
    return jax.shard_map(
        on_device,
        mesh=split,
        in_specs=(
            P(names, toks, None),
            P(names, toks, None),
            P(),
            P(names, None),
            P(names, None),
            P(names, None),
            P(names, None),
            P(names, None),
            P(None, toks, None),
            P(),
        ),
        out_specs=(P(names, toks, None), P(None, toks, names)),
        check_vma=False,
    )
```

```python
import jax
import jax.numpy as jnp
from jax import lax
from jax.experimental import pallas as pl
from jax.experimental.pallas import tpu as pltpu
from jax.sharding import Mesh, PartitionSpec as P

AXES = (("x", 4), ("zh", 2), ("y", 4), ("core", 2))
TOK = (("th", 2), ("tl", 2))
NX, NZ, NY, NC = 4, 2, 4, 2
NT = 4
BF = jnp.bfloat16
F32 = jnp.float32
NEG = -1000000000.0


def shift(value, axis, count, by):
    return lax.ppermute(value, axis, [(i, (i + by) % count) for i in range(count)])


def swap(value, by):
    return lax.ppermute(value, ("th", "tl"), [(i, i ^ by) for i in range(NT)])


def nt(a, b):
    return lax.dot_general(a, b, (((1,), (1,)), ((), ())), preferred_element_type=F32)


def nn(a, b):
    return lax.dot_general(a, b, (((1,), (0,)), ((), ())), preferred_element_type=F32)


def attention_kernel(
    pos,
    own_near, own_far, oth_near, oth_far,
    cot_own0, cot_own1, cot_oth0, cot_oth1,
    weights,
    bias, bias_pair, valid_row,
    own_near_out, own_far_out, own_go, oth_keep, oth_go, out_bias,
    wf, wo, wb, dgt, kv, km, kvt, qt, gt, dx, dqg,
):
    heads = bias_pair.shape[0]
    width = own_near.shape[1]
    part = width // 4
    size = part // heads
    rows = bias.shape[1]
    scale = float(size) ** (-0.5)
    core, tok, pair = pos[2], pos[3], pos[5]
    rx, rz, ry = width // NX, width // (NX * NZ), width // (NX * NZ * NY)
    tail = weights.shape[2] - width

    for block in range(NX * NY):
        to_x, to_y = divmod(block, NY)
        rows_of = weights[block].astype(F32)
        for z in range(NZ):
            at = to_x * rx + z * rz + to_y * ry
            wf[at:at + ry, :] = rows_of[z * ry:(z + 1) * ry, :width]
            at = to_x * rz + to_y * ry
            wo[at:at + ry, z * tail:(z + 1) * tail] = rows_of[z * ry:(z + 1) * ry, width:]
    wb[...] = wf[...].astype(BF)

    mine = jnp.concatenate(
        [wo[pl.ds(pl.multiple_of(j * rz + pair * size, 8), size), :] for j in range(heads)], axis=0
    ).astype(BF)
    cots = jnp.concatenate([cot_own0[...], cot_own1[...], cot_oth0[...], cot_oth1[...]], axis=0)
    both = nt(mine, cots)
    for s in range(2):
        dgt[s] = both[:, 2 * s * rows:2 * (s + 1) * rows]

    starts = [pl.multiple_of((tok ^ r) * rows, rows) for r in range(NT)]
    tokens = jnp.concatenate([own_near[...], own_far[...], oth_near[...], oth_far[...]], axis=0)
    both = nn(tokens, wb[:, : 2 * part])
    keep = jnp.concatenate(
        [jnp.broadcast_to(valid_row[:, pl.ds(at, rows)], (rows, rows)).T for at in starts], axis=0
    )
    for s in range(2):
        one = both[s * NT * rows:(s + 1) * NT * rows]
        kv[s] = one.astype(BF)
        kvt[s] = one.T.astype(BF)
        for j in range(2):
            km[s, :, j * 128:(j + 1) * 128] = (one[:, j * 128:(j + 1) * 128] * keep).astype(BF)
    both = nn(jnp.concatenate([own_near[...], oth_near[...]], axis=0), wb[:, 2 * part:]).T
    for s in range(2):
        one = both[:, 2 * s * rows:2 * (s + 1) * rows]
        qt[s] = one[:part].astype(BF)
        gt[s] = jax.nn.sigmoid(one[part:].astype(BF).astype(F32))

    def widen(block, first):
        low = first // 128 * 128
        high = -(-(first + size) // 128) * 128
        parts = [block]
        if first > low:
            parts = [jnp.zeros((first - low, block.shape[1]), BF)] + parts
        if high > first + size:
            parts = parts + [jnp.zeros((high - first - size, block.shape[1]), BF)]
        return low, high, jnp.concatenate(parts, axis=0)

    for h in range(heads):
        first = h * size
        at = slice(first, first + size)
        blocks = []
        for start in starts:
            keys = pl.ds(start, rows)
            both = jnp.concatenate([bias[h, :, keys], bias_pair[h, :, keys]], axis=0)
            blocks.append(jnp.where(valid_row[:, keys] > 0.0, both.astype(F32), NEG).T)
        bias_t = jnp.concatenate(blocks, axis=0)
        total = None
        for s in range(2):
            q_h = qt[s, at, :]
            dgated = dgt[s, at, :]
            sig = gt[s, at, :]
            da_h = (dgated * sig).astype(BF)
            low, high, q_wide = widen(q_h, first)
            scores = nn(km[s, :, low:high], q_wide) * scale + bias_t
            top = jnp.max(scores, axis=0, keepdims=True)
            e = jnp.exp(scores - top)
            probs = e * (1.0 / jnp.sum(e, axis=0, keepdims=True))
            probs_b = probs.astype(BF)
            att = nn(kvt[s, part + first:part + first + size, :], probs_b).astype(BF).astype(F32)
            delta = jnp.sum(da_h.astype(F32) * att, axis=0, keepdims=True)
            low, high, da_wide = widen(da_h, part + first)
            d_prob = nn(kv[s, :, low:high], da_wide)
            d_score = probs * (d_prob - delta)
            total = d_score if total is None else total + d_score
            ds_b = d_score.astype(BF)
            dqg[s, at, :] = (nn(kvt[s, at, :], ds_b) * scale).astype(BF)
            dqg[s, part + first:part + first + size, :] = (dgated * att * sig * (1.0 - sig)).astype(BF)
            dx[s, at, :] = (nt(q_h, ds_b) * scale).astype(BF)
            dx[s, part + first:part + first + size, :] = nt(da_h, probs_b).astype(BF)
        each = rows // (NZ * NY)
        for r in range(NT):
            for z in range(NZ):
                for to_y in range(NY):
                    lo = r * rows + z * (rows // NZ) + to_y * each
                    out_bias[(tok ^ r) * NY + to_y, h, z] = total[lo:lo + each, :].astype(BF)

    for s in range(2):
        wide = 2 * rows
        near = nn(wb[...], jnp.concatenate([dx[s, :, :wide], dqg[s]], axis=0))
        far = nn(wb[:, : 2 * part], dx[s, :, wide:])
        go = own_go if s == 0 else oth_go
        go[0] = near[:, rows:].astype(BF)
        go[1] = far[:, rows:].astype(BF)
        if s == 0:
            own_near_out[...] = near[:, :rows]
            own_far_out[...] = far[:, :rows]
        else:
            oth_keep[0] = near[:, :rows].astype(BF)
            oth_keep[1] = far[:, :rows].astype(BF)


def pack_kernel(pos, query, key, value, gate, out, mine, send):
    width = query.shape[1]
    part = width // 4
    size = part // NX
    row = lax.broadcasted_iota(jnp.int32, (width, part), 0)
    lane = lax.broadcasted_iota(jnp.int32, (width, part), 1)
    col = lane + pos[5] * size
    for k in range(1, NX):
        col = col + jnp.where(lane >= k * size, width // NX - size, 0)
    low = jnp.where(row == col, 1.0, 0.0).astype(BF)
    high = jnp.where(row == col + 2 * size, 1.0, 0.0).astype(BF)
    first = pos[2] == 0
    lows = jnp.concatenate([nn(w[...], low) for w in (key, value, query, gate)], axis=1)
    highs = jnp.concatenate([nn(w[...], high) for w in (key, value, query, gate)], axis=1)
    mine[:, :width] = jnp.where(first, lows, highs).astype(BF)
    send[:, :width] = jnp.where(first, highs, lows).astype(BF)
    mine[:, width:] = out[...]
    send[:, width:] = out[...]


def norm_kernel(inputs, gain, normed):
    xf = inputs[...].astype(F32)
    centered = xf - jnp.mean(xf, axis=-1, keepdims=True)
    inv = lax.rsqrt(jnp.mean(centered * centered, axis=-1, keepdims=True) + 1e-05)
    normed[...] = (centered * inv * gain[...][None, :]).astype(BF)


def assemble_kernel(pos, mine, beside, above, across, normed, beyond, part, near):
    rows = normed.shape[0]
    near[:rows, :] = normed[...]
    near[rows:, :] = beyond[...]
    first, below = pos[2] == 0, pos[4] == 0
    m, b, u, d = (ref[...].astype(F32) for ref in (mine, beside, above, across))
    near_lo, near_hi = jnp.where(first, m, b), jnp.where(first, b, m)
    far_lo, far_hi = jnp.where(first, u, d), jnp.where(first, d, u)
    cols = normed.shape[1]
    half = part.shape[2] - cols
    quad = jnp.concatenate(
        [
            jnp.where(below, near_lo, far_lo)[:, :cols],
            jnp.where(below, near_hi, far_hi)[:, :cols],
            jnp.where(below, far_lo, near_lo)[:, :cols],
            jnp.where(below, far_hi, near_hi)[:, :cols],
        ],
        axis=0,
    ).astype(BF)
    same = pos[4] == pos[2]
    out_lo, out_hi = jnp.where(same, near_lo, far_lo), jnp.where(same, near_hi, far_hi)
    tail = jnp.concatenate(
        [out_lo[:, cols:cols + half], out_hi[:, cols:cols + half], out_lo[:, cols + half:], out_hi[:, cols + half:]], axis=0
    ).astype(BF)
    for k in range(part.shape[0]):
        part[k, :, :cols] = quad
        part[k, :, cols:] = tail


def sum_kernel(own, oth, out):
    out[...] = (own[...].astype(F32) + oth[...].astype(F32)).astype(BF)


def halve_kernel(own_near, own_far, oth, got, near, far):
    near[...] = own_near[...] + oth[0].astype(F32) + got[0].astype(F32)
    far[...] = (own_far[...] + oth[1].astype(F32) + got[1].astype(F32)).astype(BF)


def plane_kernel(pos, parts, after, out):
    rows = out.shape[-1]
    each = out.shape[-2]
    total = jnp.sum(parts[...].astype(F32), axis=0)
    for z in range(NZ):
        for c in range(NC):
            for u in range(2):
                block = total[:, z, c * each:(c + 1) * each, u * rows:(u + 1) * rows]
                out[z, c, pos[5] ^ u] = block.astype(BF)


def final_kernel(inputs, gain, near, back, out):
    d = near[...] + back[...].astype(F32)
    g = d.T * gain[...][None, :]
    xf = inputs[...].astype(F32)
    mean = jnp.mean(xf, axis=-1, keepdims=True)
    centered = xf - mean
    inv = lax.rsqrt(jnp.mean(centered * centered, axis=-1, keepdims=True) + 1e-05)
    xhat = centered * inv
    res = inv * (g - jnp.mean(g, axis=-1, keepdims=True) - xhat * jnp.mean(g * xhat, axis=-1, keepdims=True))
    out[...] = res.astype(BF)


def on_device(
    inputs,
    cotangent,
    layer_norm_scale,
    query_weight,
    key_weight,
    value_weight,
    gate_weight,
    out_weight,
    pair_bias,
    atom_count,
):
    x, zh, y, core, th, tl = (lax.axis_index(a) for a in ("x", "zh", "y", "core", "th", "tl"))
    inputs, cotangent = inputs[0], cotangent[0]
    rows, width = inputs.shape
    part = width // 4
    heads = pair_bias.shape[0] // 4
    total = pair_bias.shape[2]

    pos = jnp.stack([x, y, core, 2 * th + tl, zh, tl]).astype(jnp.int32)
    vmem = pl.BlockSpec(memory_space=pltpu.VMEM)
    smem = pl.BlockSpec(memory_space=pltpu.SMEM)
    anywhere = pl.BlockSpec(memory_space=pl.ANY)
    gain = layer_norm_scale
    room = pltpu.CompilerParams(vmem_limit_bytes=58 * 1024 * 1024)

    packed = jax.ShapeDtypeStruct((query_weight.shape[0], 2 * width), BF)
    mine, send = pl.pallas_call(
        pack_kernel,
        out_shape=(packed, packed),
        in_specs=[smem] + [vmem] * 5,
        out_specs=(vmem, vmem),
        name="pack",
    )(pos, query_weight, key_weight, value_weight, gate_weight, out_weight)
    beside = shift(send, "core", NC, 1)
    above = shift(mine, "zh", NZ, 1)
    across = lax.ppermute(send, ("zh", "core"), [(0, 3), (3, 0), (1, 2), (2, 1)])

    normed = pl.pallas_call(
        norm_kernel,
        out_shape=jax.ShapeDtypeStruct((rows, width), BF),
        in_specs=[vmem, vmem],
        out_specs=vmem,
        name="norm",
    )(inputs, gain)
    beyond = swap(normed, 1)

    pieces, own_near = pl.pallas_call(
        assemble_kernel,
        out_shape=(
            jax.ShapeDtypeStruct((NX * NY, NC * NZ * mine.shape[0], width + width // 2), BF),
            jax.ShapeDtypeStruct((2 * rows, width), BF),
        ),
        in_specs=[smem] + [vmem] * 6,
        out_specs=(vmem, vmem),
        compiler_params=room,
        name="assemble",
    )(pos, mine, beside, above, across, normed, beyond)
    own_far = swap(own_near, 2)
    weights = lax.all_to_all(pieces, ("x", "y"), 0, 0, tiled=True)
    oth_near, oth_far = shift(own_near, "core", NC, 1), shift(own_far, "core", NC, 1)
    cot_pair = swap(cotangent, 1)
    cots = [cotangent, cot_pair, shift(cotangent, "core", NC, 1), shift(cot_pair, "core", NC, 1)]
    groups = pair_bias.reshape((heads, NC, 2) + pair_bias.shape[1:])
    groups = lax.dynamic_index_in_dim(groups, core, 1, False)
    theirs = lax.dynamic_index_in_dim(groups, 1 - tl, 1, False)
    bias_mine = lax.dynamic_index_in_dim(groups, tl, 1, False)
    bias_pair = swap(theirs, 1)

    valid = (atom_count > 0).astype(F32)
    operands = [own_near, own_far, oth_near, oth_far] + cots + [weights]
    operands += [bias_mine, bias_pair, valid[None, :]]
    own_near_out, own_far_out, own_go, oth_keep, oth_go, out_bias = pl.pallas_call(
        attention_kernel,
        out_shape=(
            jax.ShapeDtypeStruct((width, rows), F32),
            jax.ShapeDtypeStruct((width, rows), F32),
            jax.ShapeDtypeStruct((2, width, rows), BF),
            jax.ShapeDtypeStruct((2, width, rows), BF),
            jax.ShapeDtypeStruct((2, width, rows), BF),
            jax.ShapeDtypeStruct((NX * NY, heads, NZ, rows // (NZ * NY), 2 * rows), BF),
        ),
        in_specs=[smem] + [vmem] * len(operands),
        out_specs=(vmem,) * 6,
        scratch_shapes=[
            pltpu.VMEM((width, width), F32),
            pltpu.VMEM((width // 2, width), F32),
            pltpu.VMEM((width, width), BF),
            pltpu.VMEM((2, part, 2 * rows), F32),
            pltpu.VMEM((2, total, 2 * part), BF),
            pltpu.VMEM((2, total, 256), BF),
            pltpu.VMEM((2, 2 * part, total), BF),
            pltpu.VMEM((2, part, 2 * rows), BF),
            pltpu.VMEM((2, part, 2 * rows), F32),
            pltpu.VMEM((2, 2 * part, total), BF),
            pltpu.VMEM((2, 2 * part, 2 * rows), BF),
        ],
        compiler_params=room,
        name="attention",
    )(pos, *operands)

    go = pl.pallas_call(
        sum_kernel,
        out_shape=jax.ShapeDtypeStruct((2, width, rows), BF),
        in_specs=[vmem, vmem],
        out_specs=vmem,
        compiler_params=room,
        name="sum_cores",
    )(own_go, shift(oth_go, "core", NC, 1))
    near, far = pl.pallas_call(
        halve_kernel,
        out_shape=(jax.ShapeDtypeStruct((width, rows), F32), jax.ShapeDtypeStruct((width, rows), BF)),
        in_specs=[vmem] * 4,
        out_specs=(vmem, vmem),
        compiler_params=room,
        name="sum_pair",
    )(own_near_out, own_far_out, shift(oth_keep, "core", NC, 1), swap(go, 1))
    back = swap(far, 2)

    parts = lax.all_to_all(out_bias, ("x", "y"), 0, 0, tiled=True)
    planes = pl.pallas_call(
        plane_kernel,
        out_shape=jax.ShapeDtypeStruct((NZ, NC, 2, heads, rows // (NZ * NY) // NC, rows), BF),
        in_specs=[smem, vmem, anywhere],
        out_specs=vmem,
        compiler_params=room,
        name="sum_plane",
    )(pos, parts, far)
    shape = planes.shape
    planes = lax.all_to_all(planes.reshape((-1,) + shape[3:]), ("zh", "core", "tl"), 0, 0, tiled=True)
    planes = jnp.sum(planes.reshape(shape).astype(F32), axis=0)
    bias_grad = jnp.transpose(planes, (2, 0, 1, 4, 3)).reshape(4 * heads, rows, shape[4])

    input_grad = pl.pallas_call(
        final_kernel,
        out_shape=jax.ShapeDtypeStruct((rows, width), BF),
        in_specs=[vmem] * 4,
        out_specs=vmem,
        compiler_params=room,
        name="norm_back",
    )(inputs, gain, near, back)
    return input_grad[None], bias_grad


def solution(mesh):
    names, toks = tuple(name for name, _ in AXES), tuple(name for name, _ in TOK)
    split = Mesh(mesh.devices.reshape(tuple(n for _, n in AXES + TOK)), names + toks)
    return jax.shard_map(
        on_device,
        mesh=split,
        in_specs=(
            P(names, toks, None),
            P(names, toks, None),
            P(),
            P(names, None),
            P(names, None),
            P(names, None),
            P(names, None),
            P(names, None),
            P(None, toks, None),
            P(),
        ),
        out_specs=(P(names, toks, None), P(None, toks, names)),
        check_vma=False,
    )
```

```python
import jax
import jax.numpy as jnp
from jax import lax
from jax.experimental import pallas as pl
from jax.experimental.pallas import tpu as pltpu
from jax.sharding import Mesh, PartitionSpec as P

AXES = (("x", 4), ("zh", 2), ("y", 4), ("core", 2))
TOK = (("th", 2), ("tl", 2))
NX, NZ, NY, NC = 4, 2, 4, 2
NT = 4
BF = jnp.bfloat16
F32 = jnp.float32
NEG = -1000000000.0


def shift(value, axis, count, by):
    return lax.ppermute(value, axis, [(i, (i + by) % count) for i in range(count)])


def swap(value, by):
    return lax.ppermute(value, ("th", "tl"), [(i, i ^ by) for i in range(NT)])


def nt(a, b):
    return lax.dot_general(a, b, (((1,), (1,)), ((), ())), preferred_element_type=F32)


def nn(a, b):
    return lax.dot_general(a, b, (((1,), (0,)), ((), ())), preferred_element_type=F32)


def attention_kernel(
    pos,
    own_near, own_far, oth_near, oth_far,
    cot_own0, cot_own1, cot_oth0, cot_oth1,
    weights,
    bias, bias_pair, valid_row,
    own_near_out, own_far_out, own_go, oth_keep, oth_go, out_bias,
    wf, wo, wb, dgt, kv, km, kvt, qt, gt, dx, dqg,
):
    heads = bias_pair.shape[0]
    width = own_near.shape[1]
    part = width // 4
    size = part // heads
    rows = bias.shape[1]
    scale = float(size) ** (-0.5)
    core, tok, pair = pos[2], pos[3], pos[5]
    rx, rz, ry = width // NX, width // (NX * NZ), width // (NX * NZ * NY)
    tail = weights.shape[2] - width

    for block in range(NX * NY):
        to_x, to_y = divmod(block, NY)
        rows_of = weights[block].astype(F32)
        for z in range(NZ):
            at = to_x * rx + z * rz + to_y * ry
            wf[at:at + ry, :] = rows_of[z * ry:(z + 1) * ry, :width]
            at = to_x * rz + to_y * ry
            wo[at:at + ry, z * tail:(z + 1) * tail] = rows_of[z * ry:(z + 1) * ry, width:]
    wb[...] = wf[...].astype(BF)

    mine = jnp.concatenate(
        [wo[pl.ds(pl.multiple_of(j * rz + pair * size, 8), size), :] for j in range(heads)], axis=0
    ).astype(BF)
    cots = jnp.concatenate([cot_own0[...], cot_own1[...], cot_oth0[...], cot_oth1[...]], axis=0)
    both = nt(mine, cots)
    for s in range(2):
        dgt[s] = both[:, 2 * s * rows:2 * (s + 1) * rows]

    starts = [pl.multiple_of((tok ^ r) * rows, rows) for r in range(NT)]
    tokens = jnp.concatenate([own_near[...], own_far[...], oth_near[...], oth_far[...]], axis=0)
    both = nn(tokens, wb[:, : 2 * part])
    keep = jnp.concatenate(
        [jnp.broadcast_to(valid_row[:, pl.ds(at, rows)], (rows, rows)).T for at in starts], axis=0
    )
    for s in range(2):
        one = both[s * NT * rows:(s + 1) * NT * rows]
        kv[s] = one.astype(BF)
        kvt[s] = one.T.astype(BF)
        for j in range(2):
            km[s, :, j * 128:(j + 1) * 128] = (one[:, j * 128:(j + 1) * 128] * keep).astype(BF)
    both = nn(jnp.concatenate([own_near[...], oth_near[...]], axis=0), wb[:, 2 * part:]).T
    for s in range(2):
        one = both[:, 2 * s * rows:2 * (s + 1) * rows]
        qt[s] = one[:part].astype(BF)
        gt[s] = jax.nn.sigmoid(one[part:].astype(BF).astype(F32))

    def widen(block, first):
        low = first // 128 * 128
        high = -(-(first + size) // 128) * 128
        parts = [block]
        if first > low:
            parts = [jnp.zeros((first - low, block.shape[1]), BF)] + parts
        if high > first + size:
            parts = parts + [jnp.zeros((high - first - size, block.shape[1]), BF)]
        return low, high, jnp.concatenate(parts, axis=0)

    for h in range(heads):
        first = h * size
        at = slice(first, first + size)
        blocks = []
        for start in starts:
            keys = pl.ds(start, rows)
            both = jnp.concatenate([bias[h, :, keys], bias_pair[h, :, keys]], axis=0)
            blocks.append(jnp.where(valid_row[:, keys] > 0.0, both.astype(F32), NEG).T)
        bias_t = jnp.concatenate(blocks, axis=0)
        total = None
        for s in range(2):
            q_h = qt[s, at, :]
            dgated = dgt[s, at, :]
            sig = gt[s, at, :]
            da_h = (dgated * sig).astype(BF)
            low, high, q_wide = widen(q_h, first)
            scores = nn(km[s, :, low:high], q_wide) * scale + bias_t
            top = jnp.max(scores, axis=0, keepdims=True)
            e = jnp.exp(scores - top)
            probs = e * (1.0 / jnp.sum(e, axis=0, keepdims=True))
            probs_b = probs.astype(BF)
            att = nn(kvt[s, part + first:part + first + size, :], probs_b).astype(BF).astype(F32)
            delta = jnp.sum(da_h.astype(F32) * att, axis=0, keepdims=True)
            low, high, da_wide = widen(da_h, part + first)
            d_prob = nn(kv[s, :, low:high], da_wide)
            d_score = probs * (d_prob - delta)
            total = d_score if total is None else total + d_score
            ds_b = d_score.astype(BF)
            dqg[s, at, :] = (nn(kvt[s, at, :], ds_b) * scale).astype(BF)
            dqg[s, part + first:part + first + size, :] = (dgated * att * sig * (1.0 - sig)).astype(BF)
            dx[s, at, :] = (nt(q_h, ds_b) * scale).astype(BF)
            dx[s, part + first:part + first + size, :] = nt(da_h, probs_b).astype(BF)
        each = rows // (NZ * NY)
        for r in range(NT):
            for z in range(NZ):
                for to_y in range(NY):
                    lo = r * rows + z * (rows // NZ) + to_y * each
                    out_bias[(tok ^ r) * NY + to_y, h, z] = total[lo:lo + each, :].astype(BF)

    for s in range(2):
        wide = 2 * rows
        near = nn(wb[...], jnp.concatenate([dx[s, :, :wide], dqg[s]], axis=0))
        far = nn(wb[:, : 2 * part], dx[s, :, wide:])
        go = own_go if s == 0 else oth_go
        go[0] = near[:, rows:].astype(BF)
        go[1] = far[:, rows:].astype(BF)
        if s == 0:
            own_near_out[...] = near[:, :rows]
            own_far_out[...] = far[:, :rows]
        else:
            oth_keep[0] = near[:, :rows].astype(BF)
            oth_keep[1] = far[:, :rows].astype(BF)


def pack_kernel(pos, query, key, value, gate, out, mine, send):
    width = query.shape[1]
    part = width // 4
    size = part // NX
    row = lax.broadcasted_iota(jnp.int32, (width, part), 0)
    lane = lax.broadcasted_iota(jnp.int32, (width, part), 1)
    col = lane + pos[5] * size
    for k in range(1, NX):
        col = col + jnp.where(lane >= k * size, width // NX - size, 0)
    low = jnp.where(row == col, 1.0, 0.0).astype(BF)
    high = jnp.where(row == col + 2 * size, 1.0, 0.0).astype(BF)
    first = pos[2] == 0
    lows = jnp.concatenate([nn(w[...], low) for w in (key, value, query, gate)], axis=1)
    highs = jnp.concatenate([nn(w[...], high) for w in (key, value, query, gate)], axis=1)
    mine[:, :width] = jnp.where(first, lows, highs).astype(BF)
    send[:, :width] = jnp.where(first, highs, lows).astype(BF)
    mine[:, width:] = out[...]
    send[:, width:] = out[...]


def norm_kernel(inputs, gain, normed):
    xf = inputs[...].astype(F32)
    centered = xf - jnp.mean(xf, axis=-1, keepdims=True)
    inv = lax.rsqrt(jnp.mean(centered * centered, axis=-1, keepdims=True) + 1e-05)
    normed[...] = (centered * inv * gain[...][None, :]).astype(BF)


def assemble_kernel(pos, mine, beside, above, across, normed, beyond, after, ready, part, near):
    rows = normed.shape[0]
    near[:rows, :] = normed[...]
    near[rows:, :] = beyond[...]
    first, below = pos[2] == 0, pos[4] == 0
    m, b, u, d = (ref[...].astype(F32) for ref in (mine, beside, above, across))
    near_lo, near_hi = jnp.where(first, m, b), jnp.where(first, b, m)
    far_lo, far_hi = jnp.where(first, u, d), jnp.where(first, d, u)
    cols = normed.shape[1]
    half = part.shape[2] - cols
    quad = jnp.concatenate(
        [
            jnp.where(below, near_lo, far_lo)[:, :cols],
            jnp.where(below, near_hi, far_hi)[:, :cols],
            jnp.where(below, far_lo, near_lo)[:, :cols],
            jnp.where(below, far_hi, near_hi)[:, :cols],
        ],
        axis=0,
    ).astype(BF)
    same = pos[4] == pos[2]
    out_lo, out_hi = jnp.where(same, near_lo, far_lo), jnp.where(same, near_hi, far_hi)
    tail = jnp.concatenate(
        [out_lo[:, cols:cols + half], out_hi[:, cols:cols + half], out_lo[:, cols + half:], out_hi[:, cols + half:]], axis=0
    ).astype(BF)
    for k in range(part.shape[0]):
        part[k, :, :cols] = quad
        part[k, :, cols:] = tail


def sum_kernel(own, oth, out):
    out[...] = (own[...].astype(F32) + oth[...].astype(F32)).astype(BF)


def halve_kernel(own_near, own_far, oth, got, near, far):
    near[...] = own_near[...] + oth[0].astype(F32) + got[0].astype(F32)
    far[...] = (own_far[...] + oth[1].astype(F32) + got[1].astype(F32)).astype(BF)


def plane_kernel(pos, parts, after, out):
    rows = out.shape[-1]
    each = out.shape[-2]
    total = jnp.sum(parts[...].astype(F32), axis=0)
    for z in range(NZ):
        for c in range(NC):
            for u in range(2):
                block = total[:, z, c * each:(c + 1) * each, u * rows:(u + 1) * rows]
                out[z, c, pos[5] ^ u] = block.astype(BF)


def final_kernel(inputs, gain, near, back, out):
    d = near[...] + back[...].astype(F32)
    g = d.T * gain[...][None, :]
    xf = inputs[...].astype(F32)
    mean = jnp.mean(xf, axis=-1, keepdims=True)
    centered = xf - mean
    inv = lax.rsqrt(jnp.mean(centered * centered, axis=-1, keepdims=True) + 1e-05)
    xhat = centered * inv
    res = inv * (g - jnp.mean(g, axis=-1, keepdims=True) - xhat * jnp.mean(g * xhat, axis=-1, keepdims=True))
    out[...] = res.astype(BF)


def on_device(
    inputs,
    cotangent,
    layer_norm_scale,
    query_weight,
    key_weight,
    value_weight,
    gate_weight,
    out_weight,
    pair_bias,
    atom_count,
):
    x, zh, y, core, th, tl = (lax.axis_index(a) for a in ("x", "zh", "y", "core", "th", "tl"))
    inputs, cotangent = inputs[0], cotangent[0]
    rows, width = inputs.shape
    part = width // 4
    heads = pair_bias.shape[0] // 4
    total = pair_bias.shape[2]

    pos = jnp.stack([x, y, core, 2 * th + tl, zh, tl]).astype(jnp.int32)
    vmem = pl.BlockSpec(memory_space=pltpu.VMEM)
    smem = pl.BlockSpec(memory_space=pltpu.SMEM)
    anywhere = pl.BlockSpec(memory_space=pl.ANY)
    gain = layer_norm_scale
    room = pltpu.CompilerParams(vmem_limit_bytes=58 * 1024 * 1024)

    groups = pair_bias.reshape((heads, NC, 2) + pair_bias.shape[1:])
    groups = lax.dynamic_index_in_dim(groups, core, 1, False)
    theirs = lax.dynamic_index_in_dim(groups, 1 - tl, 1, False)
    bias_mine = lax.dynamic_index_in_dim(groups, tl, 1, False)

    packed = jax.ShapeDtypeStruct((query_weight.shape[0], 2 * width), BF)
    mine, send = pl.pallas_call(
        pack_kernel,
        out_shape=(packed, packed),
        in_specs=[smem] + [vmem] * 5,
        out_specs=(vmem, vmem),
        name="pack",
    )(pos, query_weight, key_weight, value_weight, gate_weight, out_weight)
    beside = shift(send, "core", NC, 1)
    above = shift(mine, "zh", NZ, 1)
    across = lax.ppermute(send, ("zh", "core"), [(0, 3), (3, 0), (1, 2), (2, 1)])

    normed = pl.pallas_call(
        norm_kernel,
        out_shape=jax.ShapeDtypeStruct((rows, width), BF),
        in_specs=[vmem, vmem],
        out_specs=vmem,
        name="norm",
    )(inputs, gain)
    beyond = swap(normed, 1)
    cot_pair = swap(cotangent, 1)

    pieces, own_near = pl.pallas_call(
        assemble_kernel,
        out_shape=(
            jax.ShapeDtypeStruct((NX * NY, NC * NZ * mine.shape[0], width + width // 2), BF),
            jax.ShapeDtypeStruct((2 * rows, width), BF),
        ),
        in_specs=[smem] + [vmem] * 6 + [anywhere] * 2,
        out_specs=(vmem, vmem),
        compiler_params=room,
        name="assemble",
    )(pos, mine, beside, above, across, normed, beyond, cot_pair, theirs)
    own_far = swap(own_near, 2)
    weights = lax.all_to_all(pieces, ("x", "y"), 0, 0, tiled=True)
    oth_near, oth_far = shift(own_near, "core", NC, 1), shift(own_far, "core", NC, 1)
    cots = [cotangent, cot_pair, shift(cotangent, "core", NC, 1), shift(cot_pair, "core", NC, 1)]
    bias_pair = swap(theirs, 1)

    valid = (atom_count > 0).astype(F32)
    operands = [own_near, own_far, oth_near, oth_far] + cots + [weights]
    operands += [bias_mine, bias_pair, valid[None, :]]
    own_near_out, own_far_out, own_go, oth_keep, oth_go, out_bias = pl.pallas_call(
        attention_kernel,
        out_shape=(
            jax.ShapeDtypeStruct((width, rows), F32),
            jax.ShapeDtypeStruct((width, rows), F32),
            jax.ShapeDtypeStruct((2, width, rows), BF),
            jax.ShapeDtypeStruct((2, width, rows), BF),
            jax.ShapeDtypeStruct((2, width, rows), BF),
            jax.ShapeDtypeStruct((NX * NY, heads, NZ, rows // (NZ * NY), 2 * rows), BF),
        ),
        in_specs=[smem] + [vmem] * len(operands),
        out_specs=(vmem,) * 6,
        scratch_shapes=[
            pltpu.VMEM((width, width), F32),
            pltpu.VMEM((width // 2, width), F32),
            pltpu.VMEM((width, width), BF),
            pltpu.VMEM((2, part, 2 * rows), F32),
            pltpu.VMEM((2, total, 2 * part), BF),
            pltpu.VMEM((2, total, 256), BF),
            pltpu.VMEM((2, 2 * part, total), BF),
            pltpu.VMEM((2, part, 2 * rows), BF),
            pltpu.VMEM((2, part, 2 * rows), F32),
            pltpu.VMEM((2, 2 * part, total), BF),
            pltpu.VMEM((2, 2 * part, 2 * rows), BF),
        ],
        compiler_params=room,
        name="attention",
    )(pos, *operands)

    go = pl.pallas_call(
        sum_kernel,
        out_shape=jax.ShapeDtypeStruct((2, width, rows), BF),
        in_specs=[vmem, vmem],
        out_specs=vmem,
        compiler_params=room,
        name="sum_cores",
    )(own_go, shift(oth_go, "core", NC, 1))
    near, far = pl.pallas_call(
        halve_kernel,
        out_shape=(jax.ShapeDtypeStruct((width, rows), F32), jax.ShapeDtypeStruct((width, rows), BF)),
        in_specs=[vmem] * 4,
        out_specs=(vmem, vmem),
        compiler_params=room,
        name="sum_pair",
    )(own_near_out, own_far_out, shift(oth_keep, "core", NC, 1), swap(go, 1))
    back = swap(far, 2)

    parts = lax.all_to_all(out_bias, ("x", "y"), 0, 0, tiled=True)
    planes = pl.pallas_call(
        plane_kernel,
        out_shape=jax.ShapeDtypeStruct((NZ, NC, 2, heads, rows // (NZ * NY) // NC, rows), BF),
        in_specs=[smem, vmem, anywhere],
        out_specs=vmem,
        compiler_params=room,
        name="sum_plane",
    )(pos, parts, far)
    shape = planes.shape
    planes = lax.all_to_all(planes.reshape((-1,) + shape[3:]), ("zh", "core", "tl"), 0, 0, tiled=True)
    planes = jnp.sum(planes.reshape(shape).astype(F32), axis=0)
    bias_grad = jnp.transpose(planes, (2, 0, 1, 4, 3)).reshape(4 * heads, rows, shape[4])

    input_grad = pl.pallas_call(
        final_kernel,
        out_shape=jax.ShapeDtypeStruct((rows, width), BF),
        in_specs=[vmem] * 4,
        out_specs=vmem,
        compiler_params=room,
        name="norm_back",
    )(inputs, gain, near, back)
    return input_grad[None], bias_grad


def solution(mesh):
    names, toks = tuple(name for name, _ in AXES), tuple(name for name, _ in TOK)
    split = Mesh(mesh.devices.reshape(tuple(n for _, n in AXES + TOK)), names + toks)
    return jax.shard_map(
        on_device,
        mesh=split,
        in_specs=(
            P(names, toks, None),
            P(names, toks, None),
            P(),
            P(names, None),
            P(names, None),
            P(names, None),
            P(names, None),
            P(names, None),
            P(None, toks, None),
            P(),
        ),
        out_specs=(P(names, toks, None), P(None, toks, names)),
        check_vma=False,
    )
```

```python
import jax
import jax.numpy as jnp
from jax import lax
from jax.experimental import pallas as pl
from jax.experimental.pallas import tpu as pltpu
from jax.sharding import Mesh, PartitionSpec as P

AXES = (("x", 4), ("zh", 2), ("y", 4), ("core", 2))
TOK = (("th", 2), ("tl", 2))
NX, NZ, NY, NC = 4, 2, 4, 2
NT = 4
BF = jnp.bfloat16
F32 = jnp.float32
NEG = -1000000000.0


def shift(value, axis, count, by):
    return lax.ppermute(value, axis, [(i, (i + by) % count) for i in range(count)])


def swap(value, by):
    return lax.ppermute(value, ("th", "tl"), [(i, i ^ by) for i in range(NT)])


def nt(a, b):
    return lax.dot_general(a, b, (((1,), (1,)), ((), ())), preferred_element_type=F32)


def nn(a, b):
    return lax.dot_general(a, b, (((1,), (0,)), ((), ())), preferred_element_type=F32)


def attention_kernel(
    pos,
    own_near, own_far, oth_near, oth_far,
    cot_own0, cot_own1, cot_oth0, cot_oth1,
    weights,
    bias, bias_pair, valid_row,
    own_near_out, own_far_out, own_go, oth_keep, oth_go, out_bias,
    wf, wo, wb, dgt, kv, km, kvt, qt, gt, dx, dqg,
):
    heads = bias_pair.shape[0]
    width = own_near.shape[1]
    part = width // 4
    size = part // heads
    rows = bias.shape[1]
    scale = float(size) ** (-0.5)
    core, tok, pair = pos[2], pos[3], pos[5]
    rx, rz, ry = width // NX, width // (NX * NZ), width // (NX * NZ * NY)
    tail = weights.shape[2] - width

    for block in range(NX * NY):
        to_x, to_y = divmod(block, NY)
        rows_of = weights[block].astype(F32)
        for z in range(NZ):
            at = to_x * rx + z * rz + to_y * ry
            wf[at:at + ry, :] = rows_of[z * ry:(z + 1) * ry, :width]
            at = to_x * rz + to_y * ry
            wo[at:at + ry, z * tail:(z + 1) * tail] = rows_of[z * ry:(z + 1) * ry, width:]
    wb[...] = wf[...].astype(BF)

    mine = jnp.concatenate(
        [wo[pl.ds(pl.multiple_of(j * rz + pair * size, 8), size), :] for j in range(heads)], axis=0
    ).astype(BF)
    cots = jnp.concatenate([cot_own0[...], cot_own1[...], cot_oth0[...], cot_oth1[...]], axis=0)
    both = nt(mine, cots)
    for s in range(2):
        dgt[s] = both[:, 2 * s * rows:2 * (s + 1) * rows]

    starts = [pl.multiple_of((tok ^ r) * rows, rows) for r in range(NT)]
    tokens = jnp.concatenate([own_near[...], own_far[...], oth_near[...], oth_far[...]], axis=0)
    both = nn(tokens, wb[:, : 2 * part])
    keep = jnp.concatenate(
        [jnp.broadcast_to(valid_row[:, pl.ds(at, rows)], (rows, rows)).T for at in starts], axis=0
    )
    for s in range(2):
        one = both[s * NT * rows:(s + 1) * NT * rows]
        kv[s] = one.astype(BF)
        kvt[s] = one.T.astype(BF)
        for j in range(2):
            km[s, :, j * 128:(j + 1) * 128] = (one[:, j * 128:(j + 1) * 128] * keep).astype(BF)
    both = nn(jnp.concatenate([own_near[...], oth_near[...]], axis=0), wb[:, 2 * part:]).T
    for s in range(2):
        one = both[:, 2 * s * rows:2 * (s + 1) * rows]
        qt[s] = one[:part].astype(BF)
        gt[s] = jax.nn.sigmoid(one[part:].astype(BF).astype(F32))

    def widen(block, first):
        low = first // 128 * 128
        high = -(-(first + size) // 128) * 128
        parts = [block]
        if first > low:
            parts = [jnp.zeros((first - low, block.shape[1]), BF)] + parts
        if high > first + size:
            parts = parts + [jnp.zeros((high - first - size, block.shape[1]), BF)]
        return low, high, jnp.concatenate(parts, axis=0)

    for h in range(heads):
        first = h * size
        at = slice(first, first + size)
        blocks = []
        for start in starts:
            keys = pl.ds(start, rows)
            both = jnp.concatenate([bias[h, :, keys], bias_pair[h, :, keys]], axis=0)
            blocks.append(jnp.where(valid_row[:, keys] > 0.0, both.astype(F32), NEG).T)
        bias_t = jnp.concatenate(blocks, axis=0)
        total = None
        for s in range(2):
            q_h = qt[s, at, :]
            dgated = dgt[s, at, :]
            sig = gt[s, at, :]
            da_h = (dgated * sig).astype(BF)
            low, high, q_wide = widen(q_h, first)
            scores = nn(km[s, :, low:high], q_wide) * scale + bias_t
            top = jnp.max(scores, axis=0, keepdims=True)
            e = jnp.exp(scores - top)
            probs = e * (1.0 / jnp.sum(e, axis=0, keepdims=True))
            probs_b = probs.astype(BF)
            att = nn(kvt[s, part + first:part + first + size, :], probs_b).astype(BF).astype(F32)
            delta = jnp.sum(da_h.astype(F32) * att, axis=0, keepdims=True)
            low, high, da_wide = widen(da_h, part + first)
            d_prob = nn(kv[s, :, low:high], da_wide)
            d_score = probs * (d_prob - delta)
            total = d_score if total is None else total + d_score
            ds_b = d_score.astype(BF)
            dqg[s, at, :] = (nn(kvt[s, at, :], ds_b) * scale).astype(BF)
            dqg[s, part + first:part + first + size, :] = (dgated * att * sig * (1.0 - sig)).astype(BF)
            dx[s, at, :] = (nt(q_h, ds_b) * scale).astype(BF)
            dx[s, part + first:part + first + size, :] = nt(da_h, probs_b).astype(BF)
        each = rows // (NZ * NY)
        for r in range(NT):
            for z in range(NZ):
                for to_y in range(NY):
                    lo = r * rows + z * (rows // NZ) + to_y * each
                    out_bias[(tok ^ r) * NY + to_y, h, z] = total[lo:lo + each, :].astype(BF)

    for s in range(2):
        wide = 2 * rows
        near = nn(wb[...], jnp.concatenate([dx[s, :, :wide], dqg[s]], axis=0))
        far = nn(wb[:, : 2 * part], dx[s, :, wide:])
        go = own_go if s == 0 else oth_go
        go[0] = near[:, rows:].astype(BF)
        go[1] = far[:, rows:].astype(BF)
        if s == 0:
            own_near_out[...] = near[:, :rows]
            own_far_out[...] = far[:, :rows]
        else:
            oth_keep[0] = near[:, :rows].astype(BF)
            oth_keep[1] = far[:, :rows].astype(BF)


def pack_kernel(pos, query, key, value, gate, out, mine, send):
    width = query.shape[1]
    part = width // 4
    size = part // NX
    row = lax.broadcasted_iota(jnp.int32, (width, part), 0)
    lane = lax.broadcasted_iota(jnp.int32, (width, part), 1)
    col = lane + pos[5] * size
    for k in range(1, NX):
        col = col + jnp.where(lane >= k * size, width // NX - size, 0)
    low = jnp.where(row == col, 1.0, 0.0).astype(BF)
    high = jnp.where(row == col + 2 * size, 1.0, 0.0).astype(BF)
    first = pos[2] == 0
    lows = jnp.concatenate([nn(w[...], low) for w in (key, value, query, gate)], axis=1)
    highs = jnp.concatenate([nn(w[...], high) for w in (key, value, query, gate)], axis=1)
    mine[:, :width] = jnp.where(first, lows, highs).astype(BF)
    send[:, :width] = jnp.where(first, highs, lows).astype(BF)
    mine[:, width:] = out[...]
    send[:, width:] = out[...]


def norm_kernel(inputs, gain, normed):
    xf = inputs[...].astype(F32)
    centered = xf - jnp.mean(xf, axis=-1, keepdims=True)
    inv = lax.rsqrt(jnp.mean(centered * centered, axis=-1, keepdims=True) + 1e-05)
    normed[...] = (centered * inv * gain[...][None, :]).astype(BF)


def assemble_kernel(pos, mine, beside, above, across, normed, beyond, after, ready, part, near):
    rows = normed.shape[0]
    near[:rows, :] = normed[...]
    near[rows:, :] = beyond[...]
    first, below = pos[2] == 0, pos[4] == 0
    m, b, u, d = (ref[...].astype(F32) for ref in (mine, beside, above, across))
    near_lo, near_hi = jnp.where(first, m, b), jnp.where(first, b, m)
    far_lo, far_hi = jnp.where(first, u, d), jnp.where(first, d, u)
    cols = normed.shape[1]
    half = part.shape[2] - cols
    quad = jnp.concatenate(
        [
            jnp.where(below, near_lo, far_lo)[:, :cols],
            jnp.where(below, near_hi, far_hi)[:, :cols],
            jnp.where(below, far_lo, near_lo)[:, :cols],
            jnp.where(below, far_hi, near_hi)[:, :cols],
        ],
        axis=0,
    ).astype(BF)
    same = pos[4] == pos[2]
    out_lo, out_hi = jnp.where(same, near_lo, far_lo), jnp.where(same, near_hi, far_hi)
    tail = jnp.concatenate(
        [out_lo[:, cols:cols + half], out_hi[:, cols:cols + half], out_lo[:, cols + half:], out_hi[:, cols + half:]], axis=0
    ).astype(BF)
    for k in range(part.shape[0]):
        part[k, :, :cols] = quad
        part[k, :, cols:] = tail


def sum_kernel(own, oth, out):
    out[...] = (own[...].astype(F32) + oth[...].astype(F32)).astype(BF)


def halve_kernel(own_near, own_far, oth, got, near, far):
    near[...] = own_near[...] + oth[0].astype(F32) + got[0].astype(F32)
    far[...] = (own_far[...] + oth[1].astype(F32) + got[1].astype(F32)).astype(BF)


def plane_kernel(pos, parts, after, out):
    rows = out.shape[-1]
    each = out.shape[-2]
    total = jnp.sum(parts[...].astype(F32), axis=0)
    for z in range(NZ):
        for c in range(NC):
            for u in range(2):
                block = total[:, z, c * each:(c + 1) * each, u * rows:(u + 1) * rows]
                out[z, c, pos[5] ^ u] = block.astype(BF)


def final_kernel(inputs, gain, near, back, out):
    d = near[...] + back[...].astype(F32)
    g = d.T * gain[...][None, :]
    xf = inputs[...].astype(F32)
    mean = jnp.mean(xf, axis=-1, keepdims=True)
    centered = xf - mean
    inv = lax.rsqrt(jnp.mean(centered * centered, axis=-1, keepdims=True) + 1e-05)
    xhat = centered * inv
    res = inv * (g - jnp.mean(g, axis=-1, keepdims=True) - xhat * jnp.mean(g * xhat, axis=-1, keepdims=True))
    out[...] = res.astype(BF)


def on_device(
    inputs,
    cotangent,
    layer_norm_scale,
    query_weight,
    key_weight,
    value_weight,
    gate_weight,
    out_weight,
    pair_bias,
    atom_count,
):
    x, zh, y, core, th, tl = (lax.axis_index(a) for a in ("x", "zh", "y", "core", "th", "tl"))
    inputs, cotangent = inputs[0], cotangent[0]
    rows, width = inputs.shape
    part = width // 4
    heads = pair_bias.shape[0] // 4
    total = pair_bias.shape[2]

    pos = jnp.stack([x, y, core, 2 * th + tl, zh, tl]).astype(jnp.int32)
    vmem = pl.BlockSpec(memory_space=pltpu.VMEM)
    smem = pl.BlockSpec(memory_space=pltpu.SMEM)
    anywhere = pl.BlockSpec(memory_space=pl.ANY)
    gain = layer_norm_scale
    room = pltpu.CompilerParams(vmem_limit_bytes=63 * 1024 * 1024)

    groups = pair_bias.reshape((heads, NC, 2) + pair_bias.shape[1:])
    groups = lax.dynamic_index_in_dim(groups, core, 1, False)
    theirs = lax.dynamic_index_in_dim(groups, 1 - tl, 1, False)
    bias_mine = lax.dynamic_index_in_dim(groups, tl, 1, False)

    packed = jax.ShapeDtypeStruct((query_weight.shape[0], 2 * width), BF)
    mine, send = pl.pallas_call(
        pack_kernel,
        out_shape=(packed, packed),
        in_specs=[smem] + [vmem] * 5,
        out_specs=(vmem, vmem),
        name="pack",
    )(pos, query_weight, key_weight, value_weight, gate_weight, out_weight)
    beside = shift(send, "core", NC, 1)
    above = shift(mine, "zh", NZ, 1)
    across = lax.ppermute(send, ("zh", "core"), [(0, 3), (3, 0), (1, 2), (2, 1)])

    normed = pl.pallas_call(
        norm_kernel,
        out_shape=jax.ShapeDtypeStruct((rows, width), BF),
        in_specs=[vmem, vmem],
        out_specs=vmem,
        name="norm",
    )(inputs, gain)
    beyond = swap(normed, 1)
    cot_pair = swap(cotangent, 1)

    pieces, own_near = pl.pallas_call(
        assemble_kernel,
        out_shape=(
            jax.ShapeDtypeStruct((NX * NY, NC * NZ * mine.shape[0], width + width // 2), BF),
            jax.ShapeDtypeStruct((2 * rows, width), BF),
        ),
        in_specs=[smem] + [vmem] * 6 + [anywhere] * 2,
        out_specs=(vmem, vmem),
        compiler_params=room,
        name="assemble",
    )(pos, mine, beside, above, across, normed, beyond, cot_pair, theirs)
    own_far = swap(own_near, 2)
    weights = lax.all_to_all(pieces, ("x", "y"), 0, 0, tiled=True)
    oth_near, oth_far = shift(own_near, "core", NC, 1), shift(own_far, "core", NC, 1)
    cots = [cotangent, cot_pair, shift(cotangent, "core", NC, 1), shift(cot_pair, "core", NC, 1)]
    bias_pair = swap(theirs, 1)

    valid = (atom_count > 0).astype(F32)
    operands = [own_near, own_far, oth_near, oth_far] + cots + [weights]
    operands += [bias_mine, bias_pair, valid[None, :]]
    own_near_out, own_far_out, own_go, oth_keep, oth_go, out_bias = pl.pallas_call(
        attention_kernel,
        out_shape=(
            jax.ShapeDtypeStruct((width, rows), F32),
            jax.ShapeDtypeStruct((width, rows), F32),
            jax.ShapeDtypeStruct((2, width, rows), BF),
            jax.ShapeDtypeStruct((2, width, rows), BF),
            jax.ShapeDtypeStruct((2, width, rows), BF),
            jax.ShapeDtypeStruct((NX * NY, heads, NZ, rows // (NZ * NY), 2 * rows), BF),
        ),
        in_specs=[smem] + [vmem] * len(operands),
        out_specs=(vmem,) * 6,
        scratch_shapes=[
            pltpu.VMEM((width, width), F32),
            pltpu.VMEM((width // 2, width), F32),
            pltpu.VMEM((width, width), BF),
            pltpu.VMEM((2, part, 2 * rows), F32),
            pltpu.VMEM((2, total, 2 * part), BF),
            pltpu.VMEM((2, total, 256), BF),
            pltpu.VMEM((2, 2 * part, total), BF),
            pltpu.VMEM((2, part, 2 * rows), BF),
            pltpu.VMEM((2, part, 2 * rows), F32),
            pltpu.VMEM((2, 2 * part, total), BF),
            pltpu.VMEM((2, 2 * part, 2 * rows), BF),
        ],
        compiler_params=room,
        name="attention",
    )(pos, *operands)

    go = pl.pallas_call(
        sum_kernel,
        out_shape=jax.ShapeDtypeStruct((2, width, rows), BF),
        in_specs=[vmem, vmem],
        out_specs=vmem,
        compiler_params=room,
        name="sum_cores",
    )(own_go, shift(oth_go, "core", NC, 1))
    near, far = pl.pallas_call(
        halve_kernel,
        out_shape=(jax.ShapeDtypeStruct((width, rows), F32), jax.ShapeDtypeStruct((width, rows), BF)),
        in_specs=[vmem] * 4,
        out_specs=(vmem, vmem),
        compiler_params=room,
        name="sum_pair",
    )(own_near_out, own_far_out, shift(oth_keep, "core", NC, 1), swap(go, 1))
    back = swap(far, 2)

    parts = lax.all_to_all(out_bias, ("x", "y"), 0, 0, tiled=True)
    planes = pl.pallas_call(
        plane_kernel,
        out_shape=jax.ShapeDtypeStruct((NZ, NC, 2, heads, rows // (NZ * NY) // NC, rows), BF),
        in_specs=[smem, vmem, anywhere],
        out_specs=vmem,
        compiler_params=room,
        name="sum_plane",
    )(pos, parts, far)
    shape = planes.shape
    planes = lax.all_to_all(planes.reshape((-1,) + shape[3:]), ("zh", "core", "tl"), 0, 0, tiled=True)
    planes = jnp.sum(planes.reshape(shape).astype(F32), axis=0)
    bias_grad = jnp.transpose(planes, (2, 0, 1, 4, 3)).reshape(4 * heads, rows, shape[4])

    input_grad = pl.pallas_call(
        final_kernel,
        out_shape=jax.ShapeDtypeStruct((rows, width), BF),
        in_specs=[vmem] * 4,
        out_specs=vmem,
        compiler_params=room,
        name="norm_back",
    )(inputs, gain, near, back)
    return input_grad[None], bias_grad


def solution(mesh):
    names, toks = tuple(name for name, _ in AXES), tuple(name for name, _ in TOK)
    split = Mesh(mesh.devices.reshape(tuple(n for _, n in AXES + TOK)), names + toks)
    return jax.shard_map(
        on_device,
        mesh=split,
        in_specs=(
            P(names, toks, None),
            P(names, toks, None),
            P(),
            P(names, None),
            P(names, None),
            P(names, None),
            P(names, None),
            P(names, None),
            P(None, toks, None),
            P(),
        ),
        out_specs=(P(names, toks, None), P(None, toks, names)),
        check_vma=False,
    )
```

```python
import jax
import jax.numpy as jnp
from jax import lax
from jax.experimental import pallas as pl
from jax.experimental.pallas import tpu as pltpu
from jax.sharding import Mesh, PartitionSpec as P

AXES = (("x", 4), ("zh", 2), ("y", 4), ("core", 2))
TOK = (("th", 2), ("tl", 2))
NX, NZ, NY, NC = 4, 2, 4, 2
NT = 4
BF = jnp.bfloat16
F32 = jnp.float32
NEG = -1000000000.0


def shift(value, axis, count, by):
    return lax.ppermute(value, axis, [(i, (i + by) % count) for i in range(count)])


def swap(value, by):
    return lax.ppermute(value, ("th", "tl"), [(i, i ^ by) for i in range(NT)])


def nt(a, b):
    return lax.dot_general(a, b, (((1,), (1,)), ((), ())), preferred_element_type=F32)


def nn(a, b):
    return lax.dot_general(a, b, (((1,), (0,)), ((), ())), preferred_element_type=F32)


def attention_kernel(
    pos,
    own_near, own_far, oth_near, oth_far,
    cot_own0, cot_own1, cot_oth0, cot_oth1,
    weights,
    bias, bias_pair, valid_row,
    own_near_out, own_far_out, own_go, oth_keep, oth_go, out_bias,
    wf, wo, wb, dgt, kv, km, kvt, qt, gt, dx, dqg,
):
    heads = bias_pair.shape[0]
    width = own_near.shape[1]
    part = width // 4
    size = part // heads
    rows = bias.shape[1]
    scale = float(size) ** (-0.5)
    core, tok, pair = pos[2], pos[3], pos[5]
    rx, rz, ry = width // NX, width // (NX * NZ), width // (NX * NZ * NY)
    tail = weights.shape[2] - width

    for block in range(NX * NY):
        to_x, to_y = divmod(block, NY)
        rows_of = weights[block].astype(F32)
        for z in range(NZ):
            at = to_x * rx + z * rz + to_y * ry
            wf[at:at + ry, :] = rows_of[z * ry:(z + 1) * ry, :width]
            at = to_x * rz + to_y * ry
            wo[at:at + ry, z * tail:(z + 1) * tail] = rows_of[z * ry:(z + 1) * ry, width:]
    wb[...] = wf[...].astype(BF)

    mine = jnp.concatenate(
        [wo[pl.ds(pl.multiple_of(j * rz + pair * size, 8), size), :] for j in range(heads)], axis=0
    ).astype(BF)
    cots = jnp.concatenate([cot_own0[...], cot_own1[...], cot_oth0[...], cot_oth1[...]], axis=0)
    both = nt(mine, cots)
    for s in range(2):
        dgt[s] = both[:, 2 * s * rows:2 * (s + 1) * rows]

    starts = [pl.multiple_of((tok ^ r) * rows, rows) for r in range(NT)]
    tokens = jnp.concatenate([own_near[...], own_far[...], oth_near[...], oth_far[...]], axis=0)
    both = nn(tokens, wb[:, : 2 * part])
    keep = jnp.concatenate(
        [jnp.broadcast_to(valid_row[:, pl.ds(at, rows)], (rows, rows)).T for at in starts], axis=0
    )
    for s in range(2):
        one = both[s * NT * rows:(s + 1) * NT * rows]
        kv[s] = one.astype(BF)
        kvt[s] = one.T.astype(BF)
        for j in range(2):
            km[s, :, j * 128:(j + 1) * 128] = (one[:, j * 128:(j + 1) * 128] * keep).astype(BF)
    both = nn(jnp.concatenate([own_near[...], oth_near[...]], axis=0), wb[:, 2 * part:]).T
    for s in range(2):
        one = both[:, 2 * s * rows:2 * (s + 1) * rows]
        qt[s] = one[:part].astype(BF)
        gt[s] = jax.nn.sigmoid(one[part:].astype(BF).astype(F32))

    def widen(block, first):
        low = first // 128 * 128
        high = -(-(first + size) // 128) * 128
        parts = [block]
        if first > low:
            parts = [jnp.zeros((first - low, block.shape[1]), BF)] + parts
        if high > first + size:
            parts = parts + [jnp.zeros((high - first - size, block.shape[1]), BF)]
        return low, high, jnp.concatenate(parts, axis=0)

    for h in range(heads):
        first = h * size
        at = slice(first, first + size)
        blocks = []
        for start in starts:
            keys = pl.ds(start, rows)
            both = jnp.concatenate([bias[h, :, keys], bias_pair[h, :, keys]], axis=0)
            blocks.append(jnp.where(valid_row[:, keys] > 0.0, both.astype(F32), NEG).T)
        bias_t = jnp.concatenate(blocks, axis=0)
        total = None
        for s in range(2):
            q_h = qt[s, at, :]
            dgated = dgt[s, at, :]
            sig = gt[s, at, :]
            da_h = (dgated * sig).astype(BF)
            low, high, q_wide = widen(q_h, first)
            scores = nn(km[s, :, low:high], q_wide) * scale + bias_t
            top = jnp.max(scores, axis=0, keepdims=True)
            e = jnp.exp(scores - top)
            probs = e * (1.0 / jnp.sum(e, axis=0, keepdims=True))
            probs_b = probs.astype(BF)
            att = nn(kvt[s, part + first:part + first + size, :], probs_b).astype(BF).astype(F32)
            delta = jnp.sum(da_h.astype(F32) * att, axis=0, keepdims=True)
            low, high, da_wide = widen(da_h, part + first)
            d_prob = nn(kv[s, :, low:high], da_wide)
            d_score = probs * (d_prob - delta)
            total = d_score if total is None else total + d_score
            ds_b = d_score.astype(BF)
            dqg[s, at, :] = (nn(kvt[s, at, :], ds_b) * scale).astype(BF)
            dqg[s, part + first:part + first + size, :] = (dgated * att * sig * (1.0 - sig)).astype(BF)
            dx[s, at, :] = (nt(q_h, ds_b) * scale).astype(BF)
            dx[s, part + first:part + first + size, :] = nt(da_h, probs_b).astype(BF)
        each = rows // (NZ * NY)
        for r in range(NT):
            for z in range(NZ):
                for to_y in range(NY):
                    lo = r * rows + z * (rows // NZ) + to_y * each
                    out_bias[(tok ^ r) * NY + to_y, h, z] = total[lo:lo + each, :].astype(BF)

    for s in range(2):
        wide = 2 * rows
        near = nn(wb[...], jnp.concatenate([dx[s, :, :wide], dqg[s]], axis=0))
        far = nn(wb[:, : 2 * part], dx[s, :, wide:])
        go = own_go if s == 0 else oth_go
        go[0] = near[:, rows:].astype(BF)
        go[1] = far[:, rows:].astype(BF)
        if s == 0:
            own_near_out[...] = near[:, :rows]
            own_far_out[...] = far[:, :rows]
        else:
            oth_keep[0] = near[:, :rows].astype(BF)
            oth_keep[1] = far[:, :rows].astype(BF)


def pack_kernel(pos, query, key, value, gate, out, mine, send):
    width = query.shape[1]
    part = width // 4
    size = part // NX
    row = lax.broadcasted_iota(jnp.int32, (width, part), 0)
    lane = lax.broadcasted_iota(jnp.int32, (width, part), 1)
    col = lane + pos[5] * size
    for k in range(1, NX):
        col = col + jnp.where(lane >= k * size, width // NX - size, 0)
    low = jnp.where(row == col, 1.0, 0.0).astype(BF)
    high = jnp.where(row == col + 2 * size, 1.0, 0.0).astype(BF)
    first = pos[2] == 0
    lows = jnp.concatenate([nn(w[...], low) for w in (key, value, query, gate)], axis=1)
    highs = jnp.concatenate([nn(w[...], high) for w in (key, value, query, gate)], axis=1)
    mine[:, :width] = jnp.where(first, lows, highs).astype(BF)
    send[:, :width] = jnp.where(first, highs, lows).astype(BF)
    mine[:, width:] = out[...]
    send[:, width:] = out[...]


def norm_kernel(inputs, gain, normed):
    xf = inputs[...].astype(F32)
    centered = xf - jnp.mean(xf, axis=-1, keepdims=True)
    inv = lax.rsqrt(jnp.mean(centered * centered, axis=-1, keepdims=True) + 1e-05)
    normed[...] = (centered * inv * gain[...][None, :]).astype(BF)


def assemble_kernel(pos, mine, beside, above, across, normed, beyond, after, ready, part, near):
    rows = normed.shape[0]
    near[:rows, :] = normed[...]
    near[rows:, :] = beyond[...]
    first, below = pos[2] == 0, pos[4] == 0
    m, b, u, d = (ref[...].astype(F32) for ref in (mine, beside, above, across))
    near_lo, near_hi = jnp.where(first, m, b), jnp.where(first, b, m)
    far_lo, far_hi = jnp.where(first, u, d), jnp.where(first, d, u)
    cols = normed.shape[1]
    half = part.shape[2] - cols
    quad = jnp.concatenate(
        [
            jnp.where(below, near_lo, far_lo)[:, :cols],
            jnp.where(below, near_hi, far_hi)[:, :cols],
            jnp.where(below, far_lo, near_lo)[:, :cols],
            jnp.where(below, far_hi, near_hi)[:, :cols],
        ],
        axis=0,
    ).astype(BF)
    same = pos[4] == pos[2]
    out_lo, out_hi = jnp.where(same, near_lo, far_lo), jnp.where(same, near_hi, far_hi)
    tail = jnp.concatenate(
        [out_lo[:, cols:cols + half], out_hi[:, cols:cols + half], out_lo[:, cols + half:], out_hi[:, cols + half:]], axis=0
    ).astype(BF)
    for k in range(part.shape[0]):
        part[k, :, :cols] = quad
        part[k, :, cols:] = tail


def plane_kernel(pos, parts, after, out):
    rows = out.shape[-1]
    each = out.shape[-2]
    total = jnp.sum(parts[...].astype(F32), axis=0)
    for z in range(NZ):
        for c in range(NC):
            for u in range(2):
                block = total[:, z, c * each:(c + 1) * each, u * rows:(u + 1) * rows]
                out[z, c, pos[5] ^ u] = block.astype(BF)


def final_kernel(inputs, gain, near, back, out):
    d = near[...] + back[...].astype(F32)
    g = d.T * gain[...][None, :]
    xf = inputs[...].astype(F32)
    mean = jnp.mean(xf, axis=-1, keepdims=True)
    centered = xf - mean
    inv = lax.rsqrt(jnp.mean(centered * centered, axis=-1, keepdims=True) + 1e-05)
    xhat = centered * inv
    res = inv * (g - jnp.mean(g, axis=-1, keepdims=True) - xhat * jnp.mean(g * xhat, axis=-1, keepdims=True))
    out[...] = res.astype(BF)


def on_device(
    inputs,
    cotangent,
    layer_norm_scale,
    query_weight,
    key_weight,
    value_weight,
    gate_weight,
    out_weight,
    pair_bias,
    atom_count,
):
    x, zh, y, core, th, tl = (lax.axis_index(a) for a in ("x", "zh", "y", "core", "th", "tl"))
    inputs, cotangent = inputs[0], cotangent[0]
    rows, width = inputs.shape
    part = width // 4
    heads = pair_bias.shape[0] // 4
    total = pair_bias.shape[2]

    pos = jnp.stack([x, y, core, 2 * th + tl, zh, tl]).astype(jnp.int32)
    vmem = pl.BlockSpec(memory_space=pltpu.VMEM)
    smem = pl.BlockSpec(memory_space=pltpu.SMEM)
    anywhere = pl.BlockSpec(memory_space=pl.ANY)
    gain = layer_norm_scale
    room = pltpu.CompilerParams(vmem_limit_bytes=63 * 1024 * 1024)

    groups = pair_bias.reshape((heads, NC, 2) + pair_bias.shape[1:])
    groups = lax.dynamic_index_in_dim(groups, core, 1, False)
    theirs = lax.dynamic_index_in_dim(groups, 1 - tl, 1, False)
    bias_mine = lax.dynamic_index_in_dim(groups, tl, 1, False)

    packed = jax.ShapeDtypeStruct((query_weight.shape[0], 2 * width), BF)
    mine, send = pl.pallas_call(
        pack_kernel,
        out_shape=(packed, packed),
        in_specs=[smem] + [vmem] * 5,
        out_specs=(vmem, vmem),
        name="pack",
    )(pos, query_weight, key_weight, value_weight, gate_weight, out_weight)
    beside = shift(send, "core", NC, 1)
    above = shift(mine, "zh", NZ, 1)
    across = lax.ppermute(send, ("zh", "core"), [(0, 3), (3, 0), (1, 2), (2, 1)])

    normed = pl.pallas_call(
        norm_kernel,
        out_shape=jax.ShapeDtypeStruct((rows, width), BF),
        in_specs=[vmem, vmem],
        out_specs=vmem,
        name="norm",
    )(inputs, gain)
    beyond = swap(normed, 1)
    cot_pair = swap(cotangent, 1)

    pieces, own_near = pl.pallas_call(
        assemble_kernel,
        out_shape=(
            jax.ShapeDtypeStruct((NX * NY, NC * NZ * mine.shape[0], width + width // 2), BF),
            jax.ShapeDtypeStruct((2 * rows, width), BF),
        ),
        in_specs=[smem] + [vmem] * 6 + [anywhere] * 2,
        out_specs=(vmem, vmem),
        compiler_params=room,
        name="assemble",
    )(pos, mine, beside, above, across, normed, beyond, cot_pair, theirs)
    own_far = swap(own_near, 2)
    weights = lax.all_to_all(pieces, ("x", "y"), 0, 0, tiled=True)
    oth_near, oth_far = shift(own_near, "core", NC, 1), shift(own_far, "core", NC, 1)
    cots = [cotangent, cot_pair, shift(cotangent, "core", NC, 1), shift(cot_pair, "core", NC, 1)]
    bias_pair = swap(theirs, 1)

    valid = (atom_count > 0).astype(F32)
    operands = [own_near, own_far, oth_near, oth_far] + cots + [weights]
    operands += [bias_mine, bias_pair, valid[None, :]]
    own_near_out, own_far_out, own_go, oth_keep, oth_go, out_bias = pl.pallas_call(
        attention_kernel,
        out_shape=(
            jax.ShapeDtypeStruct((width, rows), F32),
            jax.ShapeDtypeStruct((width, rows), F32),
            jax.ShapeDtypeStruct((2, width, rows), BF),
            jax.ShapeDtypeStruct((2, width, rows), BF),
            jax.ShapeDtypeStruct((2, width, rows), BF),
            jax.ShapeDtypeStruct((NX * NY, heads, NZ, rows // (NZ * NY), 2 * rows), BF),
        ),
        in_specs=[smem] + [vmem] * len(operands),
        out_specs=(vmem,) * 6,
        scratch_shapes=[
            pltpu.VMEM((width, width), F32),
            pltpu.VMEM((width // 2, width), F32),
            pltpu.VMEM((width, width), BF),
            pltpu.VMEM((2, part, 2 * rows), F32),
            pltpu.VMEM((2, total, 2 * part), BF),
            pltpu.VMEM((2, total, 256), BF),
            pltpu.VMEM((2, 2 * part, total), BF),
            pltpu.VMEM((2, part, 2 * rows), BF),
            pltpu.VMEM((2, part, 2 * rows), F32),
            pltpu.VMEM((2, 2 * part, total), BF),
            pltpu.VMEM((2, 2 * part, 2 * rows), BF),
        ],
        compiler_params=room,
        name="attention",
    )(pos, *operands)

    go = (own_go.astype(F32) + shift(oth_go, "core", NC, 1).astype(F32)).astype(BF)
    keep, got = shift(oth_keep, "core", NC, 1), swap(go, 1)
    near = own_near_out + keep[0].astype(F32) + got[0].astype(F32)
    far = (own_far_out + keep[1].astype(F32) + got[1].astype(F32)).astype(BF)
    back = swap(far, 2)

    parts = lax.all_to_all(out_bias, ("x", "y"), 0, 0, tiled=True)
    planes = pl.pallas_call(
        plane_kernel,
        out_shape=jax.ShapeDtypeStruct((NZ, NC, 2, heads, rows // (NZ * NY) // NC, rows), BF),
        in_specs=[smem, vmem, anywhere],
        out_specs=vmem,
        compiler_params=room,
        name="sum_plane",
    )(pos, parts, far)
    shape = planes.shape
    planes = lax.all_to_all(planes.reshape((-1,) + shape[3:]), ("zh", "core", "tl"), 0, 0, tiled=True)
    planes = jnp.sum(planes.reshape(shape).astype(F32), axis=0)
    bias_grad = jnp.transpose(planes, (2, 0, 1, 4, 3)).reshape(4 * heads, rows, shape[4])

    input_grad = pl.pallas_call(
        final_kernel,
        out_shape=jax.ShapeDtypeStruct((rows, width), BF),
        in_specs=[vmem] * 4,
        out_specs=vmem,
        compiler_params=room,
        name="norm_back",
    )(inputs, gain, near, back)
    return input_grad[None], bias_grad


def solution(mesh):
    names, toks = tuple(name for name, _ in AXES), tuple(name for name, _ in TOK)
    split = Mesh(mesh.devices.reshape(tuple(n for _, n in AXES + TOK)), names + toks)
    return jax.shard_map(
        on_device,
        mesh=split,
        in_specs=(
            P(names, toks, None),
            P(names, toks, None),
            P(),
            P(names, None),
            P(names, None),
            P(names, None),
            P(names, None),
            P(names, None),
            P(None, toks, None),
            P(),
        ),
        out_specs=(P(names, toks, None), P(None, toks, names)),
        check_vma=False,
    )
```

```python
import jax
import jax.numpy as jnp
from jax import lax
from jax.experimental import pallas as pl
from jax.experimental.pallas import tpu as pltpu
from jax.sharding import Mesh, PartitionSpec as P

AXES = (("x", 4), ("zh", 2), ("y", 4), ("core", 2))
TOK = (("th", 2), ("tl", 2))
NX, NZ, NY, NC = 4, 2, 4, 2
NT = 4
BF = jnp.bfloat16
F32 = jnp.float32
NEG = -1000000000.0


def shift(value, axis, count, by):
    return lax.ppermute(value, axis, [(i, (i + by) % count) for i in range(count)])


def swap(value, by):
    return lax.ppermute(value, ("th", "tl"), [(i, i ^ by) for i in range(NT)])


def nt(a, b):
    return lax.dot_general(a, b, (((1,), (1,)), ((), ())), preferred_element_type=F32)


def nn(a, b):
    return lax.dot_general(a, b, (((1,), (0,)), ((), ())), preferred_element_type=F32)


def attention_kernel(
    pos,
    own_near, own_far, oth_near, oth_far,
    cot_own0, cot_own1, cot_oth0, cot_oth1,
    weights,
    bias, bias_pair, valid_row,
    own_near_out, own_far_out, own_go, oth_keep, oth_go, out_bias,
    wf, wo, wb, dgt, kv, km, kvt, qt, gt, dx, dqg,
):
    heads = bias_pair.shape[0]
    width = own_near.shape[1]
    part = width // 4
    size = part // heads
    rows = bias.shape[1]
    scale = float(size) ** (-0.5)
    core, tok, pair = pos[2], pos[3], pos[5]
    rx, rz, ry = width // NX, width // (NX * NZ), width // (NX * NZ * NY)
    tail = weights.shape[2] - width

    for block in range(NX * NY):
        to_x, to_y = divmod(block, NY)
        rows_of = weights[block].astype(F32)
        for z in range(NZ):
            at = to_x * rx + z * rz + to_y * ry
            wf[at:at + ry, :] = rows_of[z * ry:(z + 1) * ry, :width]
            at = to_x * rz + to_y * ry
            wo[at:at + ry, z * tail:(z + 1) * tail] = rows_of[z * ry:(z + 1) * ry, width:]
    wb[...] = wf[...].astype(BF)

    mine = jnp.concatenate(
        [wo[pl.ds(pl.multiple_of(j * rz + pair * size, 8), size), :] for j in range(heads)], axis=0
    ).astype(BF)
    cots = jnp.concatenate([cot_own0[...], cot_own1[...], cot_oth0[...], cot_oth1[...]], axis=0)
    both = nt(mine, cots)
    for s in range(2):
        dgt[s] = both[:, 2 * s * rows:2 * (s + 1) * rows]

    starts = [pl.multiple_of((tok ^ r) * rows, rows) for r in range(NT)]
    tokens = jnp.concatenate([own_near[...], own_far[...], oth_near[...], oth_far[...]], axis=0)
    both = nn(tokens, wb[:, : 2 * part])
    keep = jnp.concatenate(
        [jnp.broadcast_to(valid_row[:, pl.ds(at, rows)], (rows, rows)).T for at in starts], axis=0
    )
    for s in range(2):
        one = both[s * NT * rows:(s + 1) * NT * rows]
        kv[s] = one.astype(BF)
        kvt[s] = one.T.astype(BF)
        for j in range(2):
            km[s, :, j * 128:(j + 1) * 128] = (one[:, j * 128:(j + 1) * 128] * keep).astype(BF)
    both = nn(jnp.concatenate([own_near[...], oth_near[...]], axis=0), wb[:, 2 * part:]).T
    for s in range(2):
        one = both[:, 2 * s * rows:2 * (s + 1) * rows]
        qt[s] = one[:part].astype(BF)
        gt[s] = jax.nn.sigmoid(one[part:].astype(BF).astype(F32))

    def widen(block, first):
        low = first // 128 * 128
        high = -(-(first + size) // 128) * 128
        parts = [block]
        if first > low:
            parts = [jnp.zeros((first - low, block.shape[1]), BF)] + parts
        if high > first + size:
            parts = parts + [jnp.zeros((high - first - size, block.shape[1]), BF)]
        return low, high, jnp.concatenate(parts, axis=0)

    for h in range(heads):
        first = h * size
        at = slice(first, first + size)
        blocks = []
        for start in starts:
            keys = pl.ds(start, rows)
            both = jnp.concatenate([bias[h, :, keys], bias_pair[h, :, keys]], axis=0)
            blocks.append(jnp.where(valid_row[:, keys] > 0.0, both.astype(F32), NEG).T)
        bias_t = jnp.concatenate(blocks, axis=0)
        total = None
        for s in range(2):
            q_h = qt[s, at, :]
            dgated = dgt[s, at, :]
            sig = gt[s, at, :]
            da_h = (dgated * sig).astype(BF)
            low, high, q_wide = widen(q_h, first)
            scores = nn(km[s, :, low:high], q_wide) * scale + bias_t
            top = jnp.max(scores, axis=0, keepdims=True)
            e = jnp.exp(scores - top)
            probs = e * (1.0 / jnp.sum(e, axis=0, keepdims=True))
            probs_b = probs.astype(BF)
            att = nn(kvt[s, part + first:part + first + size, :], probs_b).astype(BF).astype(F32)
            delta = jnp.sum(da_h.astype(F32) * att, axis=0, keepdims=True)
            low, high, da_wide = widen(da_h, part + first)
            d_prob = nn(kv[s, :, low:high], da_wide)
            d_score = probs * (d_prob - delta)
            total = d_score if total is None else total + d_score
            ds_b = d_score.astype(BF)
            dqg[s, at, :] = (nn(kvt[s, at, :], ds_b) * scale).astype(BF)
            dqg[s, part + first:part + first + size, :] = (dgated * att * sig * (1.0 - sig)).astype(BF)
            dx[s, at, :] = (nt(q_h, ds_b) * scale).astype(BF)
            dx[s, part + first:part + first + size, :] = nt(da_h, probs_b).astype(BF)
        each = rows // (NZ * NY)
        for r in range(NT):
            for z in range(NZ):
                for to_y in range(NY):
                    lo = r * rows + z * (rows // NZ) + to_y * each
                    out_bias[(tok ^ r) * NY + to_y, h, z] = total[lo:lo + each, :].astype(BF)

    for s in range(2):
        wide = 2 * rows
        near = nn(wb[...], jnp.concatenate([dx[s, :, :wide], dqg[s]], axis=0))
        far = nn(wb[:, : 2 * part], dx[s, :, wide:])
        go = own_go if s == 0 else oth_go
        go[0] = near[:, rows:].astype(BF)
        go[1] = far[:, rows:].astype(BF)
        if s == 0:
            own_near_out[...] = near[:, :rows]
            own_far_out[...] = far[:, :rows]
        else:
            oth_keep[0] = near[:, :rows].astype(BF)
            oth_keep[1] = far[:, :rows].astype(BF)


def pack_kernel(pos, query, key, value, gate, out, mine, send):
    width = query.shape[1]
    part = width // 4
    size = part // NX
    row = lax.broadcasted_iota(jnp.int32, (width, part), 0)
    lane = lax.broadcasted_iota(jnp.int32, (width, part), 1)
    col = lane + pos[5] * size
    for k in range(1, NX):
        col = col + jnp.where(lane >= k * size, width // NX - size, 0)
    low = jnp.where(row == col, 1.0, 0.0).astype(BF)
    high = jnp.where(row == col + 2 * size, 1.0, 0.0).astype(BF)
    first = pos[2] == 0
    lows = jnp.concatenate([nn(w[...], low) for w in (key, value, query, gate)], axis=1)
    highs = jnp.concatenate([nn(w[...], high) for w in (key, value, query, gate)], axis=1)
    mine[:, :width] = jnp.where(first, lows, highs).astype(BF)
    send[:, :width] = jnp.where(first, highs, lows).astype(BF)
    mine[:, width:] = out[...]
    send[:, width:] = out[...]


def norm_kernel(inputs, gain, normed):
    xf = inputs[...].astype(F32)
    centered = xf - jnp.mean(xf, axis=-1, keepdims=True)
    inv = lax.rsqrt(jnp.mean(centered * centered, axis=-1, keepdims=True) + 1e-05)
    normed[...] = (centered * inv * gain[...][None, :]).astype(BF)


def assemble_kernel(pos, mine, beside, above, across, normed, beyond, after, ready, part, near):
    rows = normed.shape[0]
    near[:rows, :] = normed[...]
    near[rows:, :] = beyond[...]
    first, below = pos[2] == 0, pos[4] == 0
    m, b, u, d = (ref[...].astype(F32) for ref in (mine, beside, above, across))
    near_lo, near_hi = jnp.where(first, m, b), jnp.where(first, b, m)
    far_lo, far_hi = jnp.where(first, u, d), jnp.where(first, d, u)
    cols = normed.shape[1]
    half = part.shape[2] - cols
    quad = jnp.concatenate(
        [
            jnp.where(below, near_lo, far_lo)[:, :cols],
            jnp.where(below, near_hi, far_hi)[:, :cols],
            jnp.where(below, far_lo, near_lo)[:, :cols],
            jnp.where(below, far_hi, near_hi)[:, :cols],
        ],
        axis=0,
    ).astype(BF)
    same = pos[4] == pos[2]
    out_lo, out_hi = jnp.where(same, near_lo, far_lo), jnp.where(same, near_hi, far_hi)
    tail = jnp.concatenate(
        [out_lo[:, cols:cols + half], out_hi[:, cols:cols + half], out_lo[:, cols + half:], out_hi[:, cols + half:]], axis=0
    ).astype(BF)
    for k in range(part.shape[0]):
        part[k, :, :cols] = quad
        part[k, :, cols:] = tail


def plane_kernel(pos, parts, after, out):
    rows = out.shape[-1]
    each = out.shape[-2]
    total = jnp.sum(parts[...].astype(F32), axis=0)
    for z in range(NZ):
        for c in range(NC):
            for u in range(2):
                block = total[:, z, c * each:(c + 1) * each, u * rows:(u + 1) * rows]
                out[z, c, pos[5] ^ u] = block.astype(BF)


def final_kernel(inputs, gain, near, back, out):
    d = near[...] + back[...].astype(F32)
    g = d.T * gain[...][None, :]
    xf = inputs[...].astype(F32)
    mean = jnp.mean(xf, axis=-1, keepdims=True)
    centered = xf - mean
    inv = lax.rsqrt(jnp.mean(centered * centered, axis=-1, keepdims=True) + 1e-05)
    xhat = centered * inv
    res = inv * (g - jnp.mean(g, axis=-1, keepdims=True) - xhat * jnp.mean(g * xhat, axis=-1, keepdims=True))
    out[...] = res.astype(BF)


def on_device(
    inputs,
    cotangent,
    layer_norm_scale,
    query_weight,
    key_weight,
    value_weight,
    gate_weight,
    out_weight,
    pair_bias,
    atom_count,
):
    x, zh, y, core, th, tl = (lax.axis_index(a) for a in ("x", "zh", "y", "core", "th", "tl"))
    inputs, cotangent = inputs[0], cotangent[0]
    rows, width = inputs.shape
    part = width // 4
    heads = pair_bias.shape[0] // 4
    total = pair_bias.shape[2]

    pos = jnp.stack([x, y, core, 2 * th + tl, zh, tl]).astype(jnp.int32)
    vmem = pl.BlockSpec(memory_space=pltpu.VMEM)
    smem = pl.BlockSpec(memory_space=pltpu.SMEM)
    anywhere = pl.BlockSpec(memory_space=pl.ANY)
    gain = layer_norm_scale
    room = pltpu.CompilerParams(vmem_limit_bytes=63 * 1024 * 1024)

    groups = pair_bias.reshape((heads, NC, 2) + pair_bias.shape[1:])
    groups = lax.dynamic_index_in_dim(groups, core, 1, False)
    theirs = lax.dynamic_index_in_dim(groups, 1 - tl, 1, False)
    bias_mine = lax.dynamic_index_in_dim(groups, tl, 1, False)

    packed = jax.ShapeDtypeStruct((query_weight.shape[0], 2 * width), BF)
    mine, send = pl.pallas_call(
        pack_kernel,
        out_shape=(packed, packed),
        in_specs=[smem] + [vmem] * 5,
        out_specs=(vmem, vmem),
        compiler_params=room,
        name="pack",
    )(pos, query_weight, key_weight, value_weight, gate_weight, out_weight)
    beside = shift(send, "core", NC, 1)
    above = shift(mine, "zh", NZ, 1)
    across = lax.ppermute(send, ("zh", "core"), [(0, 3), (3, 0), (1, 2), (2, 1)])

    normed = pl.pallas_call(
        norm_kernel,
        out_shape=jax.ShapeDtypeStruct((rows, width), BF),
        in_specs=[vmem, vmem],
        out_specs=vmem,
        compiler_params=room,
        name="norm",
    )(inputs, gain)
    beyond = swap(normed, 1)
    cot_pair = swap(cotangent, 1)

    pieces, own_near = pl.pallas_call(
        assemble_kernel,
        out_shape=(
            jax.ShapeDtypeStruct((NX * NY, NC * NZ * mine.shape[0], width + width // 2), BF),
            jax.ShapeDtypeStruct((2 * rows, width), BF),
        ),
        in_specs=[smem] + [vmem] * 6 + [anywhere] * 2,
        out_specs=(vmem, vmem),
        compiler_params=room,
        name="assemble",
    )(pos, mine, beside, above, across, normed, beyond, cot_pair, theirs)
    own_far = swap(own_near, 2)
    weights = lax.all_to_all(pieces, ("x", "y"), 0, 0, tiled=True)
    oth_near, oth_far = shift(own_near, "core", NC, 1), shift(own_far, "core", NC, 1)
    cots = [cotangent, cot_pair, shift(cotangent, "core", NC, 1), shift(cot_pair, "core", NC, 1)]
    bias_pair = swap(theirs, 1)

    valid = (atom_count > 0).astype(F32)
    operands = [own_near, own_far, oth_near, oth_far] + cots + [weights]
    operands += [bias_mine, bias_pair, valid[None, :]]
    own_near_out, own_far_out, own_go, oth_keep, oth_go, out_bias = pl.pallas_call(
        attention_kernel,
        out_shape=(
            jax.ShapeDtypeStruct((width, rows), F32),
            jax.ShapeDtypeStruct((width, rows), F32),
            jax.ShapeDtypeStruct((2, width, rows), BF),
            jax.ShapeDtypeStruct((2, width, rows), BF),
            jax.ShapeDtypeStruct((2, width, rows), BF),
            jax.ShapeDtypeStruct((NX * NY, heads, NZ, rows // (NZ * NY), 2 * rows), BF),
        ),
        in_specs=[smem] + [vmem] * len(operands),
        out_specs=(vmem,) * 6,
        scratch_shapes=[
            pltpu.VMEM((width, width), F32),
            pltpu.VMEM((width // 2, width), F32),
            pltpu.VMEM((width, width), BF),
            pltpu.VMEM((2, part, 2 * rows), F32),
            pltpu.VMEM((2, total, 2 * part), BF),
            pltpu.VMEM((2, total, 256), BF),
            pltpu.VMEM((2, 2 * part, total), BF),
            pltpu.VMEM((2, part, 2 * rows), BF),
            pltpu.VMEM((2, part, 2 * rows), F32),
            pltpu.VMEM((2, 2 * part, total), BF),
            pltpu.VMEM((2, 2 * part, 2 * rows), BF),
        ],
        compiler_params=room,
        name="attention",
    )(pos, *operands)

    go = (own_go.astype(F32) + shift(oth_go, "core", NC, 1).astype(F32)).astype(BF)
    keep, got = shift(oth_keep, "core", NC, 1), swap(go, 1)
    near = own_near_out + keep[0].astype(F32) + got[0].astype(F32)
    far = (own_far_out + keep[1].astype(F32) + got[1].astype(F32)).astype(BF)
    back = swap(far, 2)

    parts = lax.all_to_all(out_bias, ("x", "y"), 0, 0, tiled=True)
    planes = pl.pallas_call(
        plane_kernel,
        out_shape=jax.ShapeDtypeStruct((NZ, NC, 2, heads, rows // (NZ * NY) // NC, rows), BF),
        in_specs=[smem, vmem, anywhere],
        out_specs=vmem,
        compiler_params=room,
        name="sum_plane",
    )(pos, parts, far)
    shape = planes.shape
    planes = lax.all_to_all(planes.reshape((-1,) + shape[3:]), ("zh", "core", "tl"), 0, 0, tiled=True)
    planes = jnp.sum(planes.reshape(shape).astype(F32), axis=0)
    bias_grad = jnp.transpose(planes, (2, 0, 1, 4, 3)).reshape(4 * heads, rows, shape[4])

    input_grad = pl.pallas_call(
        final_kernel,
        out_shape=jax.ShapeDtypeStruct((rows, width), BF),
        in_specs=[vmem] * 4,
        out_specs=vmem,
        compiler_params=room,
        name="norm_back",
    )(inputs, gain, near, back)
    return input_grad[None], bias_grad


def solution(mesh):
    names, toks = tuple(name for name, _ in AXES), tuple(name for name, _ in TOK)
    split = Mesh(mesh.devices.reshape(tuple(n for _, n in AXES + TOK)), names + toks)
    return jax.shard_map(
        on_device,
        mesh=split,
        in_specs=(
            P(names, toks, None),
            P(names, toks, None),
            P(),
            P(names, None),
            P(names, None),
            P(names, None),
            P(names, None),
            P(names, None),
            P(None, toks, None),
            P(),
        ),
        out_specs=(P(names, toks, None), P(None, toks, names)),
        check_vma=False,
    )
```
